32 devices in a mesh: outer: 16 (over z, y, x), inner: 2 (over core).
Axes of the slice: x: 2, y: 2, z: 4, core: 2. Of those that a mesh axis runs over, the one named last changes fastest.
Arguments:
- queries: bfloat16 [8192, 1024], P(('outer', 'inner')), may hold values from -64 to 64
- keys: bfloat16 [8192, 128], P(('outer', 'inner')), may hold values from -6 to 6
- values: bfloat16 [8192, 128], P(('outer', 'inner')), may hold values from -6 to 6
- block_doc: int32 [64], P(('outer', 'inner')), may hold values from 0 to 7, never falling along the last dimension, each value on 1 to 32 neighbouring positions
Outputs:
- attended: bfloat16 [8192, 1024], P(('outer', 'inner'))
The draws below stay inside these ranges and needn't reach their ends.
Inputs may be any that keep to these rules, and one draw needn't show every extreme that they name: block_doc never falls along the sequence; each document spans 1 to 32 blocks and one spans exactly 32.
All inputs are finite; a program needn't handle non-finite values.
Results may differ from the reference program's by a relative error of at most 0.012.
Values may be sent and summed in bfloat16 or wider, within the bound.
No kernel may reach another device: no remote copies, remote signals or barrier semaphores. Data moves between devices by JAX's collectives and lax.ppermute only.
A program may use at most 64 MiB of HBM per device.

```python
import math
import jax
import jax.numpy as jnp
import numpy as np
from jax import lax

HEAD_DIM = 128
HEADS = 8
BLK = 128
DOC_BLOCKS = 32
SEQ = 8192
NBLK = 64
DOCS = 8


def draw_keys(key, part):
    table = jnp.clip(jax.random.normal(jax.random.fold_in(key, 21), (SEQ, HEAD_DIM), jnp.float32), -6.0, 6.0)
    return table.astype(jnp.bfloat16)


def draw_queries(key, part):
    table = jnp.clip(jax.random.normal(jax.random.fold_in(key, 31), (SEQ, HEADS, HEAD_DIM), jnp.float32), -6.0, 6.0)
    return table.reshape(SEQ, HEADS * HEAD_DIM).astype(jnp.bfloat16)


def block_scale(stream_key, shape, cuts, least, largest):
    def one(dim, parts):
        draws = jax.random.uniform(jax.random.fold_in(jax.random.fold_in(stream_key, 6), dim), (parts,), jnp.float32, least / len(cuts), largest / len(cuts))
        return jnp.repeat(jnp.exp(draws), shape[dim] // parts).reshape((-1,) + (1,) * (len(shape) - dim - 1))

    loudness = one(*cuts[0])
    for cut in cuts[1:]:
        loudness = loudness * one(*cut)
    return loudness


def profile(number_of, total, limit, skew):
    loads = [(1 << 20) // math.isqrt(standing ** skew) + 1 for standing in range(2, number_of + 1)]
    spare, given = total - limit - (number_of - 1), [1] * (number_of - 1)
    while spare > 0:
        free = [i for i in range(number_of - 1) if given[i] < limit]
        whole, remaining = sum([loads[i] for i in free]), spare
        for i in free:
            extra = min(limit - given[i], max(1, remaining * loads[i] // whole), spare)
            given[i] = given[i] + extra
            spare = spare - extra
    return np.array([limit] + given)


def uneven_parts(stream_key, number_of, total, reach, lean):
    if number_of == 2:
        one = jax.random.randint(stream_key, (), max(1, total - reach), min(reach, total - 1) + 1)
        return jnp.stack([one, total - one])
    lengths = jnp.asarray(profile(number_of, total, reach, lean), jnp.int32)
    couples = (number_of - 1) // 2
    source_of, taker = lengths[1:1 + 2 * couples:2], lengths[2:2 + 2 * couples:2]
    slack = jnp.minimum(source_of - 1, reach - taker)
    shifted = jax.random.randint(jax.random.fold_in(stream_key, 1), (couples,), 0, 1 << 20) % (slack + 1)
    lengths = lengths.at[1:1 + 2 * couples:2].set(source_of - shifted).at[2:2 + 2 * couples:2].set(taker + shifted)
    return lengths[jax.random.permutation(jax.random.fold_in(stream_key, 2), number_of)]


def scatter_about(stream_key, extent, width, limit, shards=(), kind=jnp.bfloat16):
    entries = jax.random.normal(stream_key, extent, jnp.float32) * width
    if len(shards) > 0:
        entries = block_scale(stream_key, extent, shards, -0.22, 0.18) * entries
    return jnp.clip(entries, min=-limit, max=limit).astype(kind)


def setup_inputs(seed: int = 0) -> dict:
    arg_keys = jax.random.split(jax.random.key(seed), 5)
    return {
        "queries": draw_queries(jax.random.fold_in(arg_keys[4], 71), 0),
        "keys": draw_keys(jax.random.fold_in(arg_keys[4], 71), 0),
        "values": scatter_about(arg_keys[2], (SEQ, HEAD_DIM), 1.0, 6.0, ((0, 32),)),
        "block_doc": jnp.searchsorted(jnp.cumsum(uneven_parts(arg_keys[3], DOCS, NBLK, DOC_BLOCKS, 2)), jnp.arange(NBLK), side="right").astype(jnp.int32),
    }


MASKED = -1e+30

def reference(queries, keys, values, block_doc):
    seq_len = queries.shape[0]
    blocks = seq_len // BLK
    margin = DOC_BLOCKS - 1
    scaling = 1.0 / math.sqrt(HEAD_DIM)
    query_blocks = queries.reshape(blocks, BLK, HEADS, HEAD_DIM)
    key_blocks = jnp.concatenate([jnp.zeros((margin, BLK, HEAD_DIM), keys.dtype), keys.reshape(blocks, BLK, HEAD_DIM)], axis=0)
    value_blocks = jnp.concatenate([jnp.zeros((margin, BLK, HEAD_DIM), values.dtype), values.reshape(blocks, BLK, HEAD_DIM)], axis=0)
    doc_padded = jnp.concatenate([jnp.full((margin,), -1, jnp.int32), block_doc.astype(jnp.int32)])
    rows = jnp.arange(BLK, dtype=jnp.int32)
    causal = rows[:, None] >= rows[None, :]

    def one_block(inputs):
        query_block, index = inputs
        own_doc = lax.dynamic_index_in_dim(doc_padded, index + margin, keepdims=False)
        query_float = query_block.astype(jnp.float32)

        def visit(carried, back):
            where_key = (index + margin - back).astype(jnp.int32)
            key_doc = lax.dynamic_index_in_dim(doc_padded, where_key, keepdims=False)

            def update(running):
                accumulated, row_max, row_sum = running
                key_block = lax.dynamic_index_in_dim(key_blocks, where_key, keepdims=False).astype(jnp.float32)
                value_block = lax.dynamic_index_in_dim(value_blocks, where_key, keepdims=False).astype(jnp.float32)
                allowed = jnp.logical_or(back > 0, causal)
                scores = jnp.einsum('qhd,kd->hqk', query_float, key_block) * scaling
                scores = jnp.where(allowed[None], scores, MASKED)
                new_max = jnp.maximum(row_max, scores.max(axis=-1))
                weights = jnp.where(allowed[None], jnp.exp(scores - new_max[..., None]), 0.0)
                factor = jnp.exp(row_max - new_max)
                row_sum = row_sum * factor + weights.sum(axis=-1)
                rounded = lax.optimization_barrier(weights.astype(jnp.bfloat16)).astype(jnp.float32)
                accumulated = accumulated * factor[..., None] + jnp.einsum('hqk,kd->hqd', rounded, value_block)
                return (accumulated, new_max, row_sum)
            return (lax.cond(key_doc == own_doc, update, lambda running: running, carried), None)
        start = (jnp.zeros((HEADS, BLK, HEAD_DIM), jnp.float32), jnp.full((HEADS, BLK), MASKED, jnp.float32), jnp.zeros((HEADS, BLK), jnp.float32))
        final, unused = lax.scan(visit, start, jnp.arange(DOC_BLOCKS, dtype=jnp.int32))
        accumulated, row_max, row_sum = final
        output = accumulated / row_sum[..., None]
        return jnp.transpose(output, (1, 0, 2)).reshape(BLK, HEADS * HEAD_DIM).astype(jnp.bfloat16)
    outputs = lax.map(one_block, (query_blocks, jnp.arange(blocks, dtype=jnp.int32)))
    return outputs.reshape(seq_len, HEADS * HEAD_DIM)
```

```python
import functools
import math

import jax
import jax.numpy as jnp
from jax import lax
from jax.experimental import pallas as pl
from jax.experimental.pallas import tpu as pltpu
from jax.sharding import PartitionSpec as P

HEAD_DIM = 128
BLK = 128
DOC_BLOCKS = 32
AXES = ("outer", "inner")

PAIR = 2
PLANE = 8

MASKED = 1e30
SAFE_SUM = 2.0**100
TO_LOG2 = math.log2(math.e) / math.sqrt(HEAD_DIM)
DOC_ROWS = 8
ON_TRANSPOSED = (((1,), (1,)), ((), ()))


def shard_rows(tokens):
    return tokens + tokens // BLK * DOC_ROWS


def columns(head):
    return slice(head * HEAD_DIM, (head + 1) * HEAD_DIM)


def scaled_scores(query, key):
    return lax.dot_general(query, key, ON_TRANSPOSED, preferred_element_type=jnp.float32) * TO_LOG2


def shards_of(refs, tokens):
    rows = shard_rows(tokens)
    return [(ref, start) for ref in refs for start in range(0, ref.shape[0], rows)]


def keys_and_values(shards, tokens):
    keys = [ref[start : start + tokens, :HEAD_DIM] for ref, start in shards]
    values = [ref[start : start + tokens, HEAD_DIM:] for ref, start in shards]
    values = jnp.concatenate(values, axis=0)
    return jnp.concatenate(keys, axis=0), jnp.concatenate([values, jnp.ones_like(values)], axis=1)


def docs_of(shard, tokens):
    ref, start = shard
    at = [start + tokens + block * DOC_ROWS for block in range(tokens // BLK)]
    return [ref[k : k + DOC_ROWS, :HEAD_DIM].astype(jnp.float32)[:1] for k in at]


def penalties(query_shard, key_shards, tokens, usable=None):
    key_docs = [doc for shard in key_shards for doc in docs_of(shard, tokens)]
    rows = []
    for own in docs_of(query_shard, tokens):
        seen = [doc == own for doc in key_docs]
        if usable is not None:
            seen = [one & usable for one in seen]
        rows.append([jnp.where(one, 0.0, MASKED) for one in seen])
    return rows


def any_visible(rows):
    least = functools.reduce(jnp.minimum, [one for row in rows for one in row])
    return jnp.min(least) < 1.0


def weights_of(scores, top_ref, rows):
    out = []
    for query_block, row in enumerate(rows):
        at = slice(query_block * BLK, (query_block + 1) * BLK)
        top = top_ref[at]
        across = [
            jnp.exp2(scores[at, columns(k)] - (top + gap)).astype(jnp.bfloat16)
            for k, gap in enumerate(row)
        ]
        out.append(jnp.concatenate(across, axis=1))
    return jnp.concatenate(out, axis=0)


def causal_bias(shard, tokens):
    (docs,) = [docs_of(shard, tokens)]
    row = lax.broadcasted_iota(jnp.int32, (BLK, BLK), 0)
    column = lax.broadcasted_iota(jnp.int32, (BLK, BLK), 1)
    corner = jnp.where(column <= row, 0.0, -MASKED)
    out = []
    for query_block, own in enumerate(docs):
        across = []
        for block, doc in enumerate(docs):
            if block == query_block:
                across.append(corner)
            elif block < query_block:
                across.append(
                    jnp.broadcast_to(jnp.where(doc == own, 0.0, -MASKED), (BLK, BLK))
                )
            else:
                across.append(jnp.full((BLK, BLK), -MASKED, jnp.float32))
        out.append(jnp.concatenate(across, axis=1))
    return jnp.concatenate(out, axis=0)


def near_weights(scores, top, tokens):
    return jnp.concatenate(
        [
            jnp.exp2(scores[:, k : k + HEAD_DIM] - top).astype(jnp.bfloat16)
            for k in range(0, tokens, HEAD_DIM)
        ],
        axis=1,
    )


def is_later():
    position = lax.axis_index("outer") * lax.axis_size("inner") + lax.axis_index("inner")
    return position % PAIR == 1


def pack(doc_ref, keys_ref, values_ref, out_ref, doc_here, semaphores):
    tokens = keys_ref.shape[0]
    copies = [
        pltpu.make_async_copy(keys_ref, out_ref.at[:tokens, :HEAD_DIM], semaphores.at[0]),
        pltpu.make_async_copy(values_ref, out_ref.at[:tokens, HEAD_DIM:], semaphores.at[1]),
        pltpu.make_async_copy(doc_ref, doc_here, semaphores.at[2]),
    ]
    for one in copies:
        one.start()
    copies[2].wait()
    shape = (tokens // BLK * DOC_ROWS, 2 * HEAD_DIM)
    block = lax.broadcasted_iota(jnp.int32, shape, 0) // DOC_ROWS
    docs = jnp.zeros(shape, jnp.int32)
    for k in range(tokens // BLK):
        docs = jnp.where(block == k, doc_here[k] + 1, docs)
    out_ref[tokens:] = docs.astype(jnp.float32).astype(out_ref.dtype)
    copies[0].wait()
    copies[1].wait()


def first_stage(
    chip_ref, query_ref, other_query_ref, top_ref, other_top_ref, sums_ref, other_sums_ref
):
    tokens = query_ref.shape[0]
    own, other = shards_of([chip_ref], tokens)
    keys, values = keys_and_values([own, other], tokens)
    bias = causal_bias(own, tokens)
    other_bias = causal_bias(other, tokens)
    rows = penalties(own, [other], tokens, is_later())

    def reference(scores):
        top = jnp.ceil(jnp.max(scores, axis=1, keepdims=True))
        return jnp.broadcast_to(top, (tokens, HEAD_DIM))

    for head in range(query_ref.shape[1] // HEAD_DIM):
        scores = scaled_scores(query_ref[:, columns(head)], keys)
        near = scores[:, :tokens] + bias
        top = reference(near)
        top_ref[head] = top
        weights = [near_weights(near, top, tokens), weights_of(scores[:, tokens:], top, rows)]
        sums_ref[head] = jnp.dot(
            jnp.concatenate(weights, axis=1), values, preferred_element_type=jnp.float32
        )
        scores = scaled_scores(other_query_ref[:, columns(head)], keys[tokens:])
        other_top_ref[head] = reference(scores + other_bias)
    other_sums_ref[...] = jnp.zeros_like(other_sums_ref)


def add_shards(query_shard, query_ref, top_ref, ref, sums_ref):
    tokens = query_ref.shape[0]
    shards = shards_of([ref], tokens)
    rows = penalties(query_shard, shards, tokens)

    @pl.when(any_visible(rows))
    def _():
        keys, values = keys_and_values(shards, tokens)
        for head in range(query_ref.shape[1] // HEAD_DIM):
            scores = scaled_scores(query_ref[:, columns(head)], keys)
            weights = weights_of(scores, top_ref.at[head], rows)
            sums_ref[head] += jnp.dot(weights, values, preferred_element_type=jnp.float32)


def middle_stage(chip_ref, query_ref, other_query_ref, top_ref, other_top_ref, *refs):
    *fresh, _, _, sums_ref, other_sums_ref = refs
    own, other = shards_of([chip_ref], query_ref.shape[0])
    for ref in fresh:
        add_shards(own, query_ref, top_ref, ref, sums_ref)
        add_shards(other, other_query_ref, other_top_ref, ref, other_sums_ref)


def repair(query_shard, near, refs, query_ref, top_ref, sums_ref):
    tokens = query_ref.shape[0]
    heads = query_ref.shape[1] // HEAD_DIM
    largest = functools.reduce(
        jnp.maximum, [sums_ref[head, :, HEAD_DIM:] for head in range(heads)]
    )

    @pl.when(jnp.logical_not(jnp.max(largest) < SAFE_SUM))
    def _():
        far = [(shard, None) for shard in shards_of(refs, tokens)]
        if near is not None:
            far = [(near, is_later())] + far

        def one_head(head, carried):
            query = query_ref[:, pl.ds(pl.multiple_of(head * HEAD_DIM, HEAD_DIM), HEAD_DIM)]
            for shard, usable in far:
                keys, _ = keys_and_values([shard], tokens)
                rows = penalties(query_shard, [shard], tokens, usable)
                scores = scaled_scores(query, keys)
                for query_block, row in enumerate(rows):
                    some = slice(query_block * BLK, (query_block + 1) * BLK)
                    top = top_ref[head, some]
                    for k, gap in enumerate(row):
                        seen = jnp.max(scores[some, columns(k)] - gap, axis=1, keepdims=True)
                        top = jnp.maximum(top, jnp.ceil(seen))
                    top_ref[head, some] = top
            top = top_ref[head]
            sums = jnp.zeros((tokens, 2 * HEAD_DIM), jnp.float32)
            if near is not None:
                keys, values = keys_and_values([query_shard], tokens)
                scores = scaled_scores(query, keys) + causal_bias(query_shard, tokens)
                weights = near_weights(scores, top, tokens)
                sums += jnp.dot(weights, values, preferred_element_type=jnp.float32)
            for shard, usable in far:
                keys, values = keys_and_values([shard], tokens)
                rows = penalties(query_shard, [shard], tokens, usable)
                weights = weights_of(scaled_scores(query, keys), top, rows)
                sums += jnp.dot(weights, values, preferred_element_type=jnp.float32)
            sums_ref[head] = sums
            return carried

        lax.fori_loop(0, heads, one_head, 0)


def side_lanes(top_ref, sums_ref, tokens):
    lane = lax.broadcasted_iota(jnp.int32, (tokens, HEAD_DIM), 1)
    heads = top_ref.shape[0]
    out = jnp.zeros((tokens, HEAD_DIM), jnp.float32)
    for head in range(heads):
        out = jnp.where(lane == head, sums_ref[head, :, HEAD_DIM:], out)
        out = jnp.where(lane == heads + head, top_ref[head], out)
    return out


def last_of_other(chip_ref, query_ref, top_in_ref, sums_in_ref, *refs):
    *fresh, out_ref, top_ref, sums_ref = refs
    tokens = query_ref.shape[0]
    heads = query_ref.shape[1] // HEAD_DIM
    _, other = shards_of([chip_ref], tokens)
    add_shards(other, query_ref, top_ref, fresh[-1], sums_ref)
    repair(other, None, fresh, query_ref, top_ref, sums_ref)
    for head in range(heads):
        out_ref[:, columns(head)] = sums_ref[head, :, :HEAD_DIM].astype(out_ref.dtype)
    side = side_lanes(top_ref, sums_ref, tokens)
    coarse = side.astype(out_ref.dtype)
    out_ref[:, columns(heads)] = coarse
    out_ref[:, columns(heads + 1)] = (side - coarse.astype(jnp.float32)).astype(out_ref.dtype)


def last_of_own(chip_ref, query_ref, top_in_ref, sums_in_ref, *refs):
    *fresh, top_ref, sums_ref = refs
    own, other = shards_of([chip_ref], query_ref.shape[0])
    add_shards(own, query_ref, top_ref, fresh[-1], sums_ref)
    repair(own, other, fresh, query_ref, top_ref, sums_ref)


def merge(top_ref, sums_ref, got_ref, out_ref, semaphores, ready):
    tokens = got_ref.shape[0]
    heads = top_ref.shape[0]
    side = got_ref[:, columns(heads)].astype(jnp.float32)
    side = side + got_ref[:, columns(heads + 1)].astype(jnp.float32)
    mine = side_lanes(top_ref, sums_ref, tokens)
    lane = lax.broadcasted_iota(jnp.int32, (tokens, HEAD_DIM), 1)
    apart = jnp.where((lane >= heads) & (lane < 2 * heads), jnp.abs(side - mine), 0.0)
    same = jnp.max(apart) == 0.0

    def spread(lane):
        return jnp.broadcast_to(side[:, lane : lane + 1], (tokens, HEAD_DIM))

    def divide(rescaled):
        for head in range(heads):
            mixture = sums_ref[head, :, :HEAD_DIM]
            row_sum = sums_ref[head, :, HEAD_DIM:]
            got = got_ref[:, columns(head)].astype(jnp.float32)
            got_sum = spread(head)
            if rescaled:
                top = top_ref[head]
                got_top = spread(heads + head)
                highest = jnp.maximum(top, got_top)
                here, there = jnp.exp2(top - highest), jnp.exp2(got_top - highest)
                mixture, row_sum = mixture * here, row_sum * here
                got, got_sum = got * there, got_sum * there
            ready[:, columns(head)] = ((mixture + got) / (row_sum + got_sum)).astype(ready.dtype)
            one_copy(head).start()

    def one_copy(head):
        at = columns(head)
        return pltpu.make_async_copy(ready.at[:, at], out_ref.at[:, at], semaphores.at[head])

    @pl.when(same)
    def _():
        divide(False)

    @pl.when(jnp.logical_not(same))
    def _():
        divide(True)

    for head in range(heads):
        one_copy(head).wait()


VMEM = pl.BlockSpec(memory_space=pltpu.VMEM)
HBM = pl.BlockSpec(memory_space=pltpu.HBM)


def in_vmem(*arrays):
    return [pltpu.with_memory_space_constraint(one, pltpu.VMEM) for one in arrays]


def call(body, out_shape, operands, aliases=None):
    return pl.pallas_call(
        body,
        out_shape=out_shape,
        in_specs=[VMEM] * len(operands),
        out_specs=jax.tree.map(lambda _: VMEM, out_shape),
        input_output_aliases=aliases or {},
        compiler_params=pltpu.CompilerParams(vmem_limit_bytes=40 << 20),
        cost_estimate=pl.CostEstimate(flops=1, bytes_accessed=1, transcendentals=0),
        name=body.__name__,
    )(*in_vmem(*operands))


def local(queries, keys, values, block_doc):
    tokens, width = queries.shape
    heads = width // HEAD_DIM
    inner_size = lax.axis_size("inner")
    count = lax.axis_size("outer") * inner_size
    assert count % PLANE == 0 and tokens % BLK == 0
    assert (DOC_BLOCKS - 1) * BLK <= 2 * PLANE * tokens
    position = lax.axis_index("outer") * inner_size + lax.axis_index("inner")
    later = position % PAIR == 1

    def send(array, target):
        route = [(d, target(d)) for d in range(count)]
        return lax.ppermute(array, AXES, [(a, b) for a, b in route if b is not None and b < count])

    def swapped(array):
        return send(array, lambda d: d ^ 1)

    def flipped(d, flip):
        return d ^ (PAIR * flip)

    def ahead(d, flip):
        return flipped(d, flip) if flipped(d, flip) > d else None

    payload = pl.pallas_call(
        pack,
        out_shape=pltpu.VMEM((shard_rows(tokens), 2 * HEAD_DIM), keys.dtype),
        in_specs=[HBM] * 3,
        out_specs=VMEM,
        scratch_shapes=[
            pltpu.SMEM(block_doc.shape, block_doc.dtype),
            pltpu.SemaphoreType.DMA((3,)),
        ],
        name="pack",
    )(block_doc, keys, values)
    chip = jnp.concatenate([payload, swapped(payload)], axis=0)
    other_queries = swapped(queries)

    first = send(chip, lambda d: ahead(d, 1) if d % PAIR else d + PLANE)
    second = send(chip, lambda d: ahead(d, 2) if d % PAIR else None)
    two_back = send(chip, lambda d: d + 2 * PLANE if d % PAIR else None)
    third = send(chip, lambda d: ahead(d, 3) if d % PAIR else None)

    top_shape = pltpu.VMEM((heads, tokens, HEAD_DIM), jnp.float32)
    sums_shape = pltpu.VMEM((heads, tokens, 2 * HEAD_DIM), jnp.float32)
    top, other_top, sums, other_sums = call(
        first_stage,
        (top_shape, top_shape, sums_shape, sums_shape),
        (chip, queries, other_queries),
    )

    def add(sums, *fresh):
        operands = (chip, queries, other_queries, top, other_top, *fresh, *sums)
        at = len(operands) - 2
        return call(middle_stage, (sums_shape, sums_shape), operands, {at: 0, at + 1: 1})

    both = add((sums, other_sums), first)
    both = add(both, second)
    first, two_back, both = lax.optimization_barrier((first, two_back, both))
    passed = jnp.where(later, two_back, first)

    def pass_on(flip):
        return send(
            passed,
            lambda d: None if d % PAIR and flipped(d, flip) > d else flipped(d, flip),
        )

    flips = [pass_on(flip) for flip in (1, 2, 3)]
    both = add(both, third, two_back)
    both = add(both, flips[0])
    sums, other_sums = add(both, flips[1])
    received = (first, second, two_back, third, *flips)
    message, _, _ = call(
        last_of_other,
        (pltpu.VMEM((tokens, width + 2 * HEAD_DIM), queries.dtype), top_shape, sums_shape),
        (chip, other_queries, other_top, other_sums, *received),
        {2: 1, 3: 2},
    )
    got = swapped(message)
    top, sums = call(
        last_of_own,
        (top_shape, sums_shape),
        (chip, queries, top, sums, *received),
        {2: 0, 3: 1},
    )
    return pl.pallas_call(
        merge,
        out_shape=jax.ShapeDtypeStruct(queries.shape, queries.dtype),
        in_specs=[VMEM] * 3,
        out_specs=HBM,
        scratch_shapes=[
            pltpu.SemaphoreType.DMA((heads,)),
            pltpu.VMEM(queries.shape, queries.dtype),
        ],
        compiler_params=pltpu.CompilerParams(vmem_limit_bytes=40 << 20),
        name="merge",
    )(*in_vmem(top, sums, got))


def solution(mesh):
    placed = (
        P(AXES, None),
        P(AXES, None),
        P(AXES, None),
        P(AXES),
    )
    return jax.shard_map(
        local, mesh=mesh, in_specs=placed, out_specs=P(AXES, None), check_vma=False
    )
```

```python
import functools
import math

import jax
import jax.numpy as jnp
from jax import lax
from jax.experimental import pallas as pl
from jax.experimental.pallas import tpu as pltpu
from jax.sharding import PartitionSpec as P

HEAD_DIM = 128
BLK = 128
DOC_BLOCKS = 32
AXES = ("outer", "inner")

PAIR = 2
PLANE = 8

MASKED = 1e30
SAFE_SUM = 2.0**100
TO_LOG2 = math.log2(math.e) / math.sqrt(HEAD_DIM)
DOC_ROWS = 8
ON_TRANSPOSED = (((1,), (1,)), ((), ()))


def shard_rows(tokens):
    return tokens + tokens // BLK * DOC_ROWS


def columns(head):
    return slice(head * HEAD_DIM, (head + 1) * HEAD_DIM)


def scaled_scores(query, key):
    return lax.dot_general(query, key, ON_TRANSPOSED, preferred_element_type=jnp.float32) * TO_LOG2


def shards_of(refs, tokens):
    rows = shard_rows(tokens)
    return [(ref, start) for ref in refs for start in range(0, ref.shape[0], rows)]


def keys_and_values(shards, tokens):
    keys = [ref[start : start + tokens, :HEAD_DIM] for ref, start in shards]
    values = [ref[start : start + tokens, HEAD_DIM:] for ref, start in shards]
    values = jnp.concatenate(values, axis=0)
    return jnp.concatenate(keys, axis=0), jnp.concatenate([values, jnp.ones_like(values)], axis=1)


def docs_of(shard, tokens):
    ref, start = shard
    at = [start + tokens + block * DOC_ROWS for block in range(tokens // BLK)]
    return [ref[k : k + DOC_ROWS, :HEAD_DIM].astype(jnp.float32)[:1] for k in at]


def penalties(query_shard, key_shards, tokens, usable=None):
    key_docs = [doc for shard in key_shards for doc in docs_of(shard, tokens)]
    rows = []
    for own in docs_of(query_shard, tokens):
        seen = [doc == own for doc in key_docs]
        if usable is not None:
            seen = [one & usable for one in seen]
        rows.append([jnp.where(one, 0.0, MASKED) for one in seen])
    return rows


def any_visible(rows):
    least = functools.reduce(jnp.minimum, [one for row in rows for one in row])
    return jnp.min(least) < 1.0


def weights_of(scores, top_ref, rows):
    out = []
    for query_block, row in enumerate(rows):
        at = slice(query_block * BLK, (query_block + 1) * BLK)
        top = top_ref[at]
        across = [
            jnp.exp2(scores[at, columns(k)] - (top + gap)).astype(jnp.bfloat16)
            for k, gap in enumerate(row)
        ]
        out.append(jnp.concatenate(across, axis=1))
    return jnp.concatenate(out, axis=0)


def causal_bias(shard, tokens):
    (docs,) = [docs_of(shard, tokens)]
    row = lax.broadcasted_iota(jnp.int32, (BLK, BLK), 0)
    column = lax.broadcasted_iota(jnp.int32, (BLK, BLK), 1)
    corner = jnp.where(column <= row, 0.0, -MASKED)
    out = []
    for query_block, own in enumerate(docs):
        across = []
        for block, doc in enumerate(docs):
            if block == query_block:
                across.append(corner)
            elif block < query_block:
                across.append(
                    jnp.broadcast_to(jnp.where(doc == own, 0.0, -MASKED), (BLK, BLK))
                )
            else:
                across.append(jnp.full((BLK, BLK), -MASKED, jnp.float32))
        out.append(jnp.concatenate(across, axis=1))
    return jnp.concatenate(out, axis=0)


def near_weights(scores, top, tokens):
    return jnp.concatenate(
        [
            jnp.exp2(scores[:, k : k + HEAD_DIM] - top).astype(jnp.bfloat16)
            for k in range(0, tokens, HEAD_DIM)
        ],
        axis=1,
    )


def is_later():
    position = lax.axis_index("outer") * lax.axis_size("inner") + lax.axis_index("inner")
    return position % PAIR == 1


def pack(doc_ref, keys_ref, values_ref, query_ref, out_ref, query_out_ref, doc_here, semaphores):
    tokens = keys_ref.shape[0]
    copies = [
        pltpu.make_async_copy(keys_ref, out_ref.at[:tokens, :HEAD_DIM], semaphores.at[0]),
        pltpu.make_async_copy(values_ref, out_ref.at[:tokens, HEAD_DIM:], semaphores.at[1]),
        pltpu.make_async_copy(doc_ref, doc_here, semaphores.at[2]),
        pltpu.make_async_copy(query_ref, query_out_ref, semaphores.at[3]),
    ]
    for one in copies:
        one.start()
    copies[2].wait()
    shape = (tokens // BLK * DOC_ROWS, 2 * HEAD_DIM)
    block = lax.broadcasted_iota(jnp.int32, shape, 0) // DOC_ROWS
    docs = jnp.zeros(shape, jnp.int32)
    for k in range(tokens // BLK):
        docs = jnp.where(block == k, doc_here[k] + 1, docs)
    out_ref[tokens:] = docs.astype(jnp.float32).astype(out_ref.dtype)
    for k in (0, 1, 3):
        copies[k].wait()


def first_stage(
    chip_ref, query_ref, other_query_ref, top_ref, other_top_ref, sums_ref, other_sums_ref
):
    tokens = query_ref.shape[0]
    own, other = shards_of([chip_ref], tokens)
    keys, values = keys_and_values([own, other], tokens)
    bias = causal_bias(own, tokens)
    other_bias = causal_bias(other, tokens)
    rows = penalties(own, [other], tokens, is_later())

    def reference(scores):
        top = jnp.ceil(jnp.max(scores, axis=1, keepdims=True))
        return jnp.broadcast_to(top, (tokens, HEAD_DIM))

    for head in range(query_ref.shape[1] // HEAD_DIM):
        scores = scaled_scores(query_ref[:, columns(head)], keys)
        near = scores[:, :tokens] + bias
        top = reference(near)
        top_ref[head] = top
        weights = [near_weights(near, top, tokens), weights_of(scores[:, tokens:], top, rows)]
        sums_ref[head] = jnp.dot(
            jnp.concatenate(weights, axis=1), values, preferred_element_type=jnp.float32
        )
        scores = scaled_scores(other_query_ref[:, columns(head)], keys[tokens:])
        other_top_ref[head] = reference(scores + other_bias)
    other_sums_ref[...] = jnp.zeros_like(other_sums_ref)


def add_shards(query_shard, query_ref, top_ref, ref, sums_ref):
    tokens = query_ref.shape[0]
    shards = shards_of([ref], tokens)
    rows = penalties(query_shard, shards, tokens)

    @pl.when(any_visible(rows))
    def _():
        keys, values = keys_and_values(shards, tokens)
        for head in range(query_ref.shape[1] // HEAD_DIM):
            scores = scaled_scores(query_ref[:, columns(head)], keys)
            weights = weights_of(scores, top_ref.at[head], rows)
            sums_ref[head] += jnp.dot(weights, values, preferred_element_type=jnp.float32)


def middle_stage(chip_ref, query_ref, other_query_ref, top_ref, other_top_ref, *refs):
    *fresh, _, _, sums_ref, other_sums_ref = refs
    own, other = shards_of([chip_ref], query_ref.shape[0])
    for ref in fresh:
        add_shards(own, query_ref, top_ref, ref, sums_ref)
        add_shards(other, other_query_ref, other_top_ref, ref, other_sums_ref)


def repair(query_shard, near, refs, query_ref, top_ref, sums_ref):
    tokens = query_ref.shape[0]
    heads = query_ref.shape[1] // HEAD_DIM
    largest = functools.reduce(
        jnp.maximum, [sums_ref[head, :, HEAD_DIM:] for head in range(heads)]
    )

    @pl.when(jnp.logical_not(jnp.max(largest) < SAFE_SUM))
    def _():
        far = [(shard, None) for shard in shards_of(refs, tokens)]
        if near is not None:
            far = [(near, is_later())] + far

        def one_head(head, carried):
            query = query_ref[:, pl.ds(pl.multiple_of(head * HEAD_DIM, HEAD_DIM), HEAD_DIM)]
            for shard, usable in far:
                keys, _ = keys_and_values([shard], tokens)
                rows = penalties(query_shard, [shard], tokens, usable)
                scores = scaled_scores(query, keys)
                for query_block, row in enumerate(rows):
                    some = slice(query_block * BLK, (query_block + 1) * BLK)
                    top = top_ref[head, some]
                    for k, gap in enumerate(row):
                        seen = jnp.max(scores[some, columns(k)] - gap, axis=1, keepdims=True)
                        top = jnp.maximum(top, jnp.ceil(seen))
                    top_ref[head, some] = top
            top = top_ref[head]
            sums = jnp.zeros((tokens, 2 * HEAD_DIM), jnp.float32)
            if near is not None:
                keys, values = keys_and_values([query_shard], tokens)
                scores = scaled_scores(query, keys) + causal_bias(query_shard, tokens)
                weights = near_weights(scores, top, tokens)
                sums += jnp.dot(weights, values, preferred_element_type=jnp.float32)
            for shard, usable in far:
                keys, values = keys_and_values([shard], tokens)
                rows = penalties(query_shard, [shard], tokens, usable)
                weights = weights_of(scaled_scores(query, keys), top, rows)
                sums += jnp.dot(weights, values, preferred_element_type=jnp.float32)
            sums_ref[head] = sums
            return carried

        lax.fori_loop(0, heads, one_head, 0)


def side_lanes(top_ref, sums_ref, tokens):
    lane = lax.broadcasted_iota(jnp.int32, (tokens, HEAD_DIM), 1)
    heads = top_ref.shape[0]
    out = jnp.zeros((tokens, HEAD_DIM), jnp.float32)
    for head in range(heads):
        out = jnp.where(lane == head, sums_ref[head, :, HEAD_DIM:], out)
        out = jnp.where(lane == heads + head, top_ref[head], out)
    return out


def last_of_other(chip_ref, query_ref, top_in_ref, sums_in_ref, *refs):
    *fresh, out_ref, top_ref, sums_ref = refs
    tokens = query_ref.shape[0]
    heads = query_ref.shape[1] // HEAD_DIM
    _, other = shards_of([chip_ref], tokens)
    add_shards(other, query_ref, top_ref, fresh[-1], sums_ref)
    repair(other, None, fresh, query_ref, top_ref, sums_ref)
    for head in range(heads):
        out_ref[:, columns(head)] = sums_ref[head, :, :HEAD_DIM].astype(out_ref.dtype)
    side = side_lanes(top_ref, sums_ref, tokens)
    coarse = side.astype(out_ref.dtype)
    out_ref[:, columns(heads)] = coarse
    out_ref[:, columns(heads + 1)] = (side - coarse.astype(jnp.float32)).astype(out_ref.dtype)


def last_of_own(chip_ref, query_ref, top_in_ref, sums_in_ref, *refs):
    *fresh, top_ref, sums_ref = refs
    own, other = shards_of([chip_ref], query_ref.shape[0])
    add_shards(own, query_ref, top_ref, fresh[-1], sums_ref)
    repair(own, other, fresh, query_ref, top_ref, sums_ref)


def merge(top_ref, sums_ref, got_ref, out_ref, semaphores, ready):
    tokens = got_ref.shape[0]
    heads = top_ref.shape[0]
    side = got_ref[:, columns(heads)].astype(jnp.float32)
    side = side + got_ref[:, columns(heads + 1)].astype(jnp.float32)
    mine = side_lanes(top_ref, sums_ref, tokens)
    lane = lax.broadcasted_iota(jnp.int32, (tokens, HEAD_DIM), 1)
    apart = jnp.where((lane >= heads) & (lane < 2 * heads), jnp.abs(side - mine), 0.0)
    same = jnp.max(apart) == 0.0

    def spread(lane):
        return jnp.broadcast_to(side[:, lane : lane + 1], (tokens, HEAD_DIM))

    def divide(rescaled):
        for head in range(heads):
            mixture = sums_ref[head, :, :HEAD_DIM]
            row_sum = sums_ref[head, :, HEAD_DIM:]
            got = got_ref[:, columns(head)].astype(jnp.float32)
            got_sum = spread(head)
            if rescaled:
                top = top_ref[head]
                got_top = spread(heads + head)
                highest = jnp.maximum(top, got_top)
                here, there = jnp.exp2(top - highest), jnp.exp2(got_top - highest)
                mixture, row_sum = mixture * here, row_sum * here
                got, got_sum = got * there, got_sum * there
            ready[:, columns(head)] = ((mixture + got) / (row_sum + got_sum)).astype(ready.dtype)
            one_copy(head).start()

    def one_copy(head):
        at = columns(head)
        return pltpu.make_async_copy(ready.at[:, at], out_ref.at[:, at], semaphores.at[head])

    @pl.when(same)
    def _():
        divide(False)

    @pl.when(jnp.logical_not(same))
    def _():
        divide(True)

    for head in range(heads):
        one_copy(head).wait()


VMEM = pl.BlockSpec(memory_space=pltpu.VMEM)
HBM = pl.BlockSpec(memory_space=pltpu.HBM)


def in_vmem(*arrays):
    return [pltpu.with_memory_space_constraint(one, pltpu.VMEM) for one in arrays]


def call(body, out_shape, operands, aliases=None):
    return pl.pallas_call(
        body,
        out_shape=out_shape,
        in_specs=[VMEM] * len(operands),
        out_specs=jax.tree.map(lambda _: VMEM, out_shape),
        input_output_aliases=aliases or {},
        compiler_params=pltpu.CompilerParams(vmem_limit_bytes=40 << 20),
        cost_estimate=pl.CostEstimate(flops=1, bytes_accessed=1, transcendentals=0),
        name=body.__name__,
    )(*in_vmem(*operands))


def local(queries, keys, values, block_doc):
    tokens, width = queries.shape
    heads = width // HEAD_DIM
    inner_size = lax.axis_size("inner")
    count = lax.axis_size("outer") * inner_size
    assert count % PLANE == 0 and tokens % BLK == 0
    assert (DOC_BLOCKS - 1) * BLK <= 2 * PLANE * tokens

    def send(array, target):
        route = [(d, target(d)) for d in range(count)]
        return lax.ppermute(array, AXES, [(a, b) for a, b in route if b is not None and b < count])

    def swapped(array):
        return send(array, lambda d: d ^ 1)

    def flipped(d, flip):
        return d ^ (PAIR * flip)

    def ahead(d, flip):
        return flipped(d, flip) if flipped(d, flip) > d else None

    def back(d, flip):
        return flipped(d, flip) if flipped(d, flip) < d else None

    payload, queries = pl.pallas_call(
        pack,
        out_shape=(
            pltpu.VMEM((shard_rows(tokens), 2 * HEAD_DIM), keys.dtype),
            pltpu.VMEM(queries.shape, queries.dtype),
        ),
        in_specs=[HBM] * 4,
        out_specs=(VMEM, VMEM),
        scratch_shapes=[
            pltpu.SMEM(block_doc.shape, block_doc.dtype),
            pltpu.SemaphoreType.DMA((4,)),
        ],
        name="pack",
    )(block_doc, keys, values, queries)
    chip = jnp.concatenate([payload, swapped(payload)], axis=0)
    other_queries = swapped(queries)

    far = send(chip, lambda d: d + PLANE * (d % PAIR + 1))
    flips = [
        send(chip, lambda d, flip=flip: ahead(d, flip) if d % PAIR else flipped(d, flip) + PLANE)
        for flip in (1, 2, 3)
    ]

    top_shape = pltpu.VMEM((heads, tokens, HEAD_DIM), jnp.float32)
    sums_shape = pltpu.VMEM((heads, tokens, 2 * HEAD_DIM), jnp.float32)
    top, other_top, sums, other_sums = call(
        first_stage,
        (top_shape, top_shape, sums_shape, sums_shape),
        (chip, queries, other_queries),
    )

    def add(sums, *fresh):
        operands = (chip, queries, other_queries, top, other_top, *fresh, *sums)
        at = len(operands) - 2
        return call(middle_stage, (sums_shape, sums_shape), operands, {at: 0, at + 1: 1})

    far, both = lax.optimization_barrier((far, (sums, other_sums)))
    behind = [
        send(far, lambda d, flip=flip: back(d, flip) if d % PAIR else None) for flip in (1, 2, 3)
    ]
    received = (far, *flips, *behind)
    for one in received[:-2]:
        both = add(both, one)
    sums, other_sums = add(both, received[-2])
    message, _, _ = call(
        last_of_other,
        (pltpu.VMEM((tokens, width + 2 * HEAD_DIM), queries.dtype), top_shape, sums_shape),
        (chip, other_queries, other_top, other_sums, *received),
        {2: 1, 3: 2},
    )
    got = swapped(message)
    top, sums = call(
        last_of_own,
        (top_shape, sums_shape),
        (chip, queries, top, sums, *received),
        {2: 0, 3: 1},
    )
    return pl.pallas_call(
        merge,
        out_shape=jax.ShapeDtypeStruct(queries.shape, queries.dtype),
        in_specs=[VMEM] * 3,
        out_specs=HBM,
        scratch_shapes=[
            pltpu.SemaphoreType.DMA((heads,)),
            pltpu.VMEM(queries.shape, queries.dtype),
        ],
        compiler_params=pltpu.CompilerParams(vmem_limit_bytes=40 << 20),
        name="merge",
    )(*in_vmem(top, sums, got))


def solution(mesh):
    placed = (
        P(AXES, None),
        P(AXES, None),
        P(AXES, None),
        P(AXES),
    )
    return jax.shard_map(
        local, mesh=mesh, in_specs=placed, out_specs=P(AXES, None), check_vma=False
    )
```

```python
import functools
import math

import jax
import jax.numpy as jnp
from jax import lax
from jax.experimental import pallas as pl
from jax.experimental.pallas import tpu as pltpu
from jax.sharding import PartitionSpec as P

HEAD_DIM = 128
BLK = 128
DOC_BLOCKS = 32
AXES = ("outer", "inner")

PAIR = 2
PLANE = 8

MASKED = 1e30
SAFE_SUM = 2.0**100
TO_LOG2 = math.log2(math.e) / math.sqrt(HEAD_DIM)
DOC_ROWS = 8
ON_TRANSPOSED = (((1,), (1,)), ((), ()))


def shard_rows(tokens):
    return tokens + tokens // BLK * DOC_ROWS


def columns(head):
    return slice(head * HEAD_DIM, (head + 1) * HEAD_DIM)


def scaled_scores(query, key):
    return lax.dot_general(query, key, ON_TRANSPOSED, preferred_element_type=jnp.float32) * TO_LOG2


def shards_of(refs, tokens):
    rows = shard_rows(tokens)
    return [(ref, start) for ref in refs for start in range(0, ref.shape[0], rows)]


def keys_and_values(shards, tokens):
    keys = [ref[start : start + tokens, :HEAD_DIM] for ref, start in shards]
    values = [ref[start : start + tokens, HEAD_DIM:] for ref, start in shards]
    values = jnp.concatenate(values, axis=0)
    return jnp.concatenate(keys, axis=0), jnp.concatenate([values, jnp.ones_like(values)], axis=1)


def docs_of(shard, tokens):
    ref, start = shard
    at = [start + tokens + block * DOC_ROWS for block in range(tokens // BLK)]
    return [ref[k : k + DOC_ROWS, :HEAD_DIM].astype(jnp.float32)[:1] for k in at]


def penalties(query_shard, key_shards, tokens, usable=None):
    key_docs = [doc for shard in key_shards for doc in docs_of(shard, tokens)]
    rows = []
    for own in docs_of(query_shard, tokens):
        seen = [doc == own for doc in key_docs]
        if usable is not None:
            seen = [one & usable for one in seen]
        rows.append([jnp.where(one, 0.0, MASKED) for one in seen])
    return rows


def any_visible(rows):
    least = functools.reduce(jnp.minimum, [one for row in rows for one in row])
    return jnp.min(least) < 1.0


def weights_of(scores, top_ref, rows):
    out = []
    for query_block, row in enumerate(rows):
        at = slice(query_block * BLK, (query_block + 1) * BLK)
        top = top_ref[at]
        across = [
            jnp.exp2(scores[at, columns(k)] - (top + gap)).astype(jnp.bfloat16)
            for k, gap in enumerate(row)
        ]
        out.append(jnp.concatenate(across, axis=1))
    return jnp.concatenate(out, axis=0)


def causal_bias(shard, tokens):
    (docs,) = [docs_of(shard, tokens)]
    row = lax.broadcasted_iota(jnp.int32, (BLK, BLK), 0)
    column = lax.broadcasted_iota(jnp.int32, (BLK, BLK), 1)
    corner = jnp.where(column <= row, 0.0, -MASKED)
    out = []
    for query_block, own in enumerate(docs):
        across = []
        for block, doc in enumerate(docs):
            if block == query_block:
                across.append(corner)
            elif block < query_block:
                across.append(
                    jnp.broadcast_to(jnp.where(doc == own, 0.0, -MASKED), (BLK, BLK))
                )
            else:
                across.append(jnp.full((BLK, BLK), -MASKED, jnp.float32))
        out.append(jnp.concatenate(across, axis=1))
    return jnp.concatenate(out, axis=0)


def near_weights(scores, top, tokens):
    return jnp.concatenate(
        [
            jnp.exp2(scores[:, k : k + HEAD_DIM] - top).astype(jnp.bfloat16)
            for k in range(0, tokens, HEAD_DIM)
        ],
        axis=1,
    )


def is_later():
    position = lax.axis_index("outer") * lax.axis_size("inner") + lax.axis_index("inner")
    return position % PAIR == 1


def pack(doc_ref, keys_ref, values_ref, query_ref, out_ref, query_out_ref, doc_here, semaphores):
    tokens = keys_ref.shape[0]
    copies = [
        pltpu.make_async_copy(keys_ref, out_ref.at[:tokens, :HEAD_DIM], semaphores.at[0]),
        pltpu.make_async_copy(values_ref, out_ref.at[:tokens, HEAD_DIM:], semaphores.at[1]),
        pltpu.make_async_copy(doc_ref, doc_here, semaphores.at[2]),
        pltpu.make_async_copy(query_ref, query_out_ref, semaphores.at[3]),
    ]
    for one in copies:
        one.start()
    copies[2].wait()
    shape = (tokens // BLK * DOC_ROWS, 2 * HEAD_DIM)
    block = lax.broadcasted_iota(jnp.int32, shape, 0) // DOC_ROWS
    docs = jnp.zeros(shape, jnp.int32)
    for k in range(tokens // BLK):
        docs = jnp.where(block == k, doc_here[k] + 1, docs)
    out_ref[tokens:] = docs.astype(jnp.float32).astype(out_ref.dtype)
    for k in (0, 1, 3):
        copies[k].wait()


def first_stage(
    chip_ref, query_ref, other_query_ref, top_ref, other_top_ref, sums_ref, other_sums_ref
):
    tokens = query_ref.shape[0]
    own, other = shards_of([chip_ref], tokens)
    keys, values = keys_and_values([own, other], tokens)
    bias = causal_bias(own, tokens)
    other_bias = causal_bias(other, tokens)
    rows = penalties(own, [other], tokens, is_later())

    def reference(scores):
        top = jnp.ceil(jnp.max(scores, axis=1, keepdims=True))
        return jnp.broadcast_to(top, (tokens, HEAD_DIM))

    for head in range(query_ref.shape[1] // HEAD_DIM):
        scores = scaled_scores(query_ref[:, columns(head)], keys)
        near = scores[:, :tokens] + bias
        top = reference(near)
        top_ref[head] = top
        weights = [near_weights(near, top, tokens), weights_of(scores[:, tokens:], top, rows)]
        sums_ref[head] = jnp.dot(
            jnp.concatenate(weights, axis=1), values, preferred_element_type=jnp.float32
        )
        scores = scaled_scores(other_query_ref[:, columns(head)], keys[tokens:])
        other_top_ref[head] = reference(scores + other_bias)
    other_sums_ref[...] = jnp.zeros_like(other_sums_ref)


def add_shards(sets, ref):
    tokens = sets[0][1].shape[0]
    shards = shards_of([ref], tokens)
    gaps = [penalties(query_shard, shards, tokens) for query_shard, *_ in sets]

    @pl.when(any_visible([row for rows in gaps for row in rows]))
    def _():
        keys, values = keys_and_values(shards, tokens)
        for head in range(sets[0][1].shape[1] // HEAD_DIM):
            for (_, query_ref, top_ref, sums_ref), rows in zip(sets, gaps):
                scores = scaled_scores(query_ref[:, columns(head)], keys)
                weights = weights_of(scores, top_ref.at[head], rows)
                sums_ref[head] += jnp.dot(weights, values, preferred_element_type=jnp.float32)


def middle_stage(chip_ref, query_ref, other_query_ref, top_ref, other_top_ref, *refs):
    *fresh, _, _, sums_ref, other_sums_ref = refs
    own, other = shards_of([chip_ref], query_ref.shape[0])
    sets = [
        (own, query_ref, top_ref, sums_ref),
        (other, other_query_ref, other_top_ref, other_sums_ref),
    ]
    for ref in fresh:
        add_shards(sets, ref)


def repair(query_shard, near, refs, query_ref, top_ref, sums_ref):
    tokens = query_ref.shape[0]
    heads = query_ref.shape[1] // HEAD_DIM
    largest = functools.reduce(
        jnp.maximum, [sums_ref[head, :, HEAD_DIM:] for head in range(heads)]
    )

    @pl.when(jnp.logical_not(jnp.max(largest) < SAFE_SUM))
    def _():
        far = [(shard, None) for shard in shards_of(refs, tokens)]
        if near is not None:
            far = [(near, is_later())] + far

        def one_head(head, carried):
            query = query_ref[:, pl.ds(pl.multiple_of(head * HEAD_DIM, HEAD_DIM), HEAD_DIM)]
            for shard, usable in far:
                keys, _ = keys_and_values([shard], tokens)
                rows = penalties(query_shard, [shard], tokens, usable)
                scores = scaled_scores(query, keys)
                for query_block, row in enumerate(rows):
                    some = slice(query_block * BLK, (query_block + 1) * BLK)
                    top = top_ref[head, some]
                    for k, gap in enumerate(row):
                        seen = jnp.max(scores[some, columns(k)] - gap, axis=1, keepdims=True)
                        top = jnp.maximum(top, jnp.ceil(seen))
                    top_ref[head, some] = top
            top = top_ref[head]
            sums = jnp.zeros((tokens, 2 * HEAD_DIM), jnp.float32)
            if near is not None:
                keys, values = keys_and_values([query_shard], tokens)
                scores = scaled_scores(query, keys) + causal_bias(query_shard, tokens)
                weights = near_weights(scores, top, tokens)
                sums += jnp.dot(weights, values, preferred_element_type=jnp.float32)
            for shard, usable in far:
                keys, values = keys_and_values([shard], tokens)
                rows = penalties(query_shard, [shard], tokens, usable)
                weights = weights_of(scaled_scores(query, keys), top, rows)
                sums += jnp.dot(weights, values, preferred_element_type=jnp.float32)
            sums_ref[head] = sums
            return carried

        lax.fori_loop(0, heads, one_head, 0)


def side_lanes(top_ref, sums_ref, tokens):
    lane = lax.broadcasted_iota(jnp.int32, (tokens, HEAD_DIM), 1)
    heads = top_ref.shape[0]
    out = jnp.zeros((tokens, HEAD_DIM), jnp.float32)
    for head in range(heads):
        out = jnp.where(lane == head, sums_ref[head, :, HEAD_DIM:], out)
        out = jnp.where(lane == heads + head, top_ref[head], out)
    return out


def last_of_other(chip_ref, query_ref, top_in_ref, sums_in_ref, *refs):
    *fresh, out_ref, top_ref, sums_ref = refs
    tokens = query_ref.shape[0]
    heads = query_ref.shape[1] // HEAD_DIM
    _, other = shards_of([chip_ref], tokens)
    add_shards([(other, query_ref, top_ref, sums_ref)], fresh[-1])
    repair(other, None, fresh, query_ref, top_ref, sums_ref)
    for head in range(heads):
        out_ref[:, columns(head)] = sums_ref[head, :, :HEAD_DIM].astype(out_ref.dtype)
    side = side_lanes(top_ref, sums_ref, tokens)
    coarse = side.astype(out_ref.dtype)
    out_ref[:, columns(heads)] = coarse
    out_ref[:, columns(heads + 1)] = (side - coarse.astype(jnp.float32)).astype(out_ref.dtype)


def last_of_own(chip_ref, query_ref, top_in_ref, sums_in_ref, *refs):
    *fresh, top_ref, sums_ref = refs
    own, other = shards_of([chip_ref], query_ref.shape[0])
    add_shards([(own, query_ref, top_ref, sums_ref)], fresh[-1])
    repair(own, other, fresh, query_ref, top_ref, sums_ref)


def merge(top_ref, sums_ref, got_ref, out_ref, semaphores, ready):
    tokens = got_ref.shape[0]
    heads = top_ref.shape[0]
    side = got_ref[:, columns(heads)].astype(jnp.float32)
    side = side + got_ref[:, columns(heads + 1)].astype(jnp.float32)
    mine = side_lanes(top_ref, sums_ref, tokens)
    lane = lax.broadcasted_iota(jnp.int32, (tokens, HEAD_DIM), 1)
    apart = jnp.where((lane >= heads) & (lane < 2 * heads), jnp.abs(side - mine), 0.0)
    same = jnp.max(apart) == 0.0

    def spread(lane):
        return jnp.broadcast_to(side[:, lane : lane + 1], (tokens, HEAD_DIM))

    def divide(rescaled):
        for head in range(heads):
            mixture = sums_ref[head, :, :HEAD_DIM]
            row_sum = sums_ref[head, :, HEAD_DIM:]
            got = got_ref[:, columns(head)].astype(jnp.float32)
            got_sum = spread(head)
            if rescaled:
                top = top_ref[head]
                got_top = spread(heads + head)
                highest = jnp.maximum(top, got_top)
                here, there = jnp.exp2(top - highest), jnp.exp2(got_top - highest)
                mixture, row_sum = mixture * here, row_sum * here
                got, got_sum = got * there, got_sum * there
            ready[:, columns(head)] = ((mixture + got) / (row_sum + got_sum)).astype(ready.dtype)
            one_copy(head).start()

    def one_copy(head):
        at = columns(head)
        return pltpu.make_async_copy(ready.at[:, at], out_ref.at[:, at], semaphores.at[head])

    @pl.when(same)
    def _():
        divide(False)

    @pl.when(jnp.logical_not(same))
    def _():
        divide(True)

    for head in range(heads):
        one_copy(head).wait()


VMEM = pl.BlockSpec(memory_space=pltpu.VMEM)
HBM = pl.BlockSpec(memory_space=pltpu.HBM)


def in_vmem(*arrays):
    return [pltpu.with_memory_space_constraint(one, pltpu.VMEM) for one in arrays]


def call(body, out_shape, operands, aliases=None):
    return pl.pallas_call(
        body,
        out_shape=out_shape,
        in_specs=[VMEM] * len(operands),
        out_specs=jax.tree.map(lambda _: VMEM, out_shape),
        input_output_aliases=aliases or {},
        compiler_params=pltpu.CompilerParams(vmem_limit_bytes=40 << 20),
        cost_estimate=pl.CostEstimate(flops=1, bytes_accessed=1, transcendentals=0),
        name=body.__name__,
    )(*in_vmem(*operands))


def local(queries, keys, values, block_doc):
    tokens, width = queries.shape
    heads = width // HEAD_DIM
    inner_size = lax.axis_size("inner")
    count = lax.axis_size("outer") * inner_size
    assert count % PLANE == 0 and tokens % BLK == 0
    assert (DOC_BLOCKS - 1) * BLK <= 2 * PLANE * tokens
    position = lax.axis_index("outer") * inner_size + lax.axis_index("inner")
    place = position // PAIR % (PLANE // PAIR)
    later = position % PAIR == 1

    def send(array, target):
        route = [(d, target(d)) for d in range(count)]
        return lax.ppermute(array, AXES, [(a, b) for a, b in route if b is not None and b < count])

    def swapped(array):
        return send(array, lambda d: d ^ 1)

    def flipped(d, flip):
        return d ^ (PAIR * flip)

    payload, queries = pl.pallas_call(
        pack,
        out_shape=(
            pltpu.VMEM((shard_rows(tokens), 2 * HEAD_DIM), keys.dtype),
            pltpu.VMEM(queries.shape, queries.dtype),
        ),
        in_specs=[HBM] * 4,
        out_specs=(VMEM, VMEM),
        scratch_shapes=[
            pltpu.SMEM(block_doc.shape, block_doc.dtype),
            pltpu.SemaphoreType.DMA((4,)),
        ],
        name="pack",
    )(block_doc, keys, values, queries)
    chip = jnp.concatenate([payload, swapped(payload)], axis=0)
    other_queries = swapped(queries)

    def straight(d, flip):
        if d % PAIR == 0:
            return flipped(d, flip) + PLANE
        return flipped(d, flip) if flipped(d, flip) > d else flipped(d, flip) + 2 * PLANE

    far = send(chip, lambda d: straight(d, 0))
    across = send(chip, lambda d: straight(d, 3))

    top_shape = pltpu.VMEM((heads, tokens, HEAD_DIM), jnp.float32)
    sums_shape = pltpu.VMEM((heads, tokens, 2 * HEAD_DIM), jnp.float32)
    top, other_top, sums, other_sums = call(
        first_stage,
        (top_shape, top_shape, sums_shape, sums_shape),
        (chip, queries, other_queries),
    )

    def add(sums, *fresh):
        operands = (chip, queries, other_queries, top, other_top, *fresh, *sums)
        at = len(operands) - 2
        return call(middle_stage, (sums_shape, sums_shape), operands, {at: 0, at + 1: 1})

    far, both = lax.optimization_barrier((far, (sums, other_sums)))

    def beside(flip):
        passed = jnp.where(later & (place & flip == 0), chip, far)
        return send(passed, lambda d: flipped(d, flip))

    received = (far, across, beside(1), beside(2))
    for one in received[:-2]:
        both = add(both, one)
    sums, other_sums = add(both, received[-2])
    message, _, _ = call(
        last_of_other,
        (pltpu.VMEM((tokens, width + 2 * HEAD_DIM), queries.dtype), top_shape, sums_shape),
        (chip, other_queries, other_top, other_sums, *received),
        {2: 1, 3: 2},
    )
    got = swapped(message)
    top, sums = call(
        last_of_own,
        (top_shape, sums_shape),
        (chip, queries, top, sums, *received),
        {2: 0, 3: 1},
    )
    return pl.pallas_call(
        merge,
        out_shape=jax.ShapeDtypeStruct(queries.shape, queries.dtype),
        in_specs=[VMEM] * 3,
        out_specs=HBM,
        scratch_shapes=[
            pltpu.SemaphoreType.DMA((heads,)),
            pltpu.VMEM(queries.shape, queries.dtype),
        ],
        compiler_params=pltpu.CompilerParams(vmem_limit_bytes=40 << 20),
        name="merge",
    )(*in_vmem(top, sums, got))


def solution(mesh):
    placed = (
        P(AXES, None),
        P(AXES, None),
        P(AXES, None),
        P(AXES),
    )
    return jax.shard_map(
        local, mesh=mesh, in_specs=placed, out_specs=P(AXES, None), check_vma=False
    )
```

```python
import functools
import math

import jax
import jax.numpy as jnp
from jax import lax
from jax.experimental import pallas as pl
from jax.experimental.pallas import tpu as pltpu
from jax.sharding import PartitionSpec as P

HEAD_DIM = 128
BLK = 128
DOC_BLOCKS = 32
AXES = ("outer", "inner")

PAIR = 2
PLANE = 8

MASKED = 1e30
SAFE_SUM = 2.0**100
TO_LOG2 = math.log2(math.e) / math.sqrt(HEAD_DIM)
DOC_ROWS = 8
ON_TRANSPOSED = (((1,), (1,)), ((), ()))


def shard_rows(tokens):
    return 2 * tokens + tokens // BLK * DOC_ROWS


def columns(head):
    return slice(head * HEAD_DIM, (head + 1) * HEAD_DIM)


def scaled_scores(query, key):
    return lax.dot_general(query, key, ON_TRANSPOSED, preferred_element_type=jnp.float32) * TO_LOG2


def shards_of(refs, tokens):
    rows = shard_rows(tokens)
    return [(ref, start) for ref in refs for start in range(0, ref.shape[0], rows)]


def keys_and_values(shards, tokens):
    keys = [ref[start : start + tokens] for ref, start in shards]
    values = [ref[start + tokens : start + 2 * tokens] for ref, start in shards]
    values = jnp.concatenate(values, axis=0)
    return jnp.concatenate(keys, axis=0), jnp.concatenate([values, jnp.ones_like(values)], axis=1)


def docs_of(shard, tokens):
    ref, start = shard
    at = [start + 2 * tokens + block * DOC_ROWS for block in range(tokens // BLK)]
    return [ref[k : k + DOC_ROWS].astype(jnp.float32)[:1] for k in at]


def penalties(query_shard, key_shards, tokens, usable=None):
    key_docs = [doc for shard in key_shards for doc in docs_of(shard, tokens)]
    rows = []
    for own in docs_of(query_shard, tokens):
        seen = [doc == own for doc in key_docs]
        if usable is not None:
            seen = [one & usable for one in seen]
        rows.append([jnp.where(one, 0.0, MASKED) for one in seen])
    return rows


def any_visible(rows):
    least = functools.reduce(jnp.minimum, [one for row in rows for one in row])
    return jnp.min(least) < 1.0


def weights_of(scores, top_ref, rows):
    out = []
    for query_block, row in enumerate(rows):
        at = slice(query_block * BLK, (query_block + 1) * BLK)
        top = top_ref[at]
        across = [
            jnp.exp2(scores[at, columns(k)] - (top + gap)).astype(jnp.bfloat16)
            for k, gap in enumerate(row)
        ]
        out.append(jnp.concatenate(across, axis=1))
    return jnp.concatenate(out, axis=0)


def causal_bias(shard, tokens):
    (docs,) = [docs_of(shard, tokens)]
    row = lax.broadcasted_iota(jnp.int32, (BLK, BLK), 0)
    column = lax.broadcasted_iota(jnp.int32, (BLK, BLK), 1)
    corner = jnp.where(column <= row, 0.0, -MASKED)
    out = []
    for query_block, own in enumerate(docs):
        across = []
        for block, doc in enumerate(docs):
            if block == query_block:
                across.append(corner)
            elif block < query_block:
                across.append(
                    jnp.broadcast_to(jnp.where(doc == own, 0.0, -MASKED), (BLK, BLK))
                )
            else:
                across.append(jnp.full((BLK, BLK), -MASKED, jnp.float32))
        out.append(jnp.concatenate(across, axis=1))
    return jnp.concatenate(out, axis=0)


def near_weights(scores, top, tokens):
    return jnp.concatenate(
        [
            jnp.exp2(scores[:, k : k + HEAD_DIM] - top).astype(jnp.bfloat16)
            for k in range(0, tokens, HEAD_DIM)
        ],
        axis=1,
    )


def is_later():
    position = lax.axis_index("outer") * lax.axis_size("inner") + lax.axis_index("inner")
    return position % PAIR == 1


def pack(doc_ref, keys_ref, values_ref, out_ref, doc_here, semaphores):
    tokens = keys_ref.shape[0]
    copies = [
        pltpu.make_async_copy(keys_ref, out_ref.at[:tokens], semaphores.at[0]),
        pltpu.make_async_copy(values_ref, out_ref.at[tokens : 2 * tokens], semaphores.at[1]),
        pltpu.make_async_copy(doc_ref, doc_here, semaphores.at[2]),
    ]
    for one in copies:
        one.start()
    copies[2].wait()
    shape = (tokens // BLK * DOC_ROWS, HEAD_DIM)
    block = lax.broadcasted_iota(jnp.int32, shape, 0) // DOC_ROWS
    docs = jnp.zeros(shape, jnp.int32)
    for k in range(tokens // BLK):
        docs = jnp.where(block == k, doc_here[k] + 1, docs)
    out_ref[2 * tokens :] = docs.astype(jnp.float32).astype(out_ref.dtype)
    copies[0].wait()
    copies[1].wait()


def first_stage(
    chip_ref, query_ref, other_query_ref, top_ref, other_top_ref, sums_ref, other_sums_ref
):
    tokens = query_ref.shape[0]
    own, other = shards_of([chip_ref], tokens)
    keys, values = keys_and_values([own, other], tokens)
    bias = causal_bias(own, tokens)
    other_bias = causal_bias(other, tokens)
    rows = penalties(own, [other], tokens, is_later())

    def reference(scores):
        top = jnp.ceil(jnp.max(scores, axis=1, keepdims=True))
        return jnp.broadcast_to(top, (tokens, HEAD_DIM))

    for head in range(query_ref.shape[1] // HEAD_DIM):
        scores = scaled_scores(query_ref[:, columns(head)], keys)
        near = scores[:, :tokens] + bias
        top = reference(near)
        top_ref[head] = top
        weights = [near_weights(near, top, tokens), weights_of(scores[:, tokens:], top, rows)]
        sums_ref[head] = jnp.dot(
            jnp.concatenate(weights, axis=1), values, preferred_element_type=jnp.float32
        )
        scores = scaled_scores(other_query_ref[:, columns(head)], keys[tokens:])
        other_top_ref[head] = reference(scores + other_bias)
    other_sums_ref[...] = jnp.zeros_like(other_sums_ref)


def add_shards(sets, ref):
    tokens = sets[0][1].shape[0]
    shards = shards_of([ref], tokens)
    gaps = [penalties(query_shard, shards, tokens) for query_shard, *_ in sets]

    @pl.when(any_visible([row for rows in gaps for row in rows]))
    def _():
        keys, values = keys_and_values(shards, tokens)
        for head in range(sets[0][1].shape[1] // HEAD_DIM):
            for (_, query_ref, top_ref, sums_ref), rows in zip(sets, gaps):
                scores = scaled_scores(query_ref[:, columns(head)], keys)
                weights = weights_of(scores, top_ref.at[head], rows)
                sums_ref[head] += jnp.dot(weights, values, preferred_element_type=jnp.float32)


def middle_stage(chip_ref, query_ref, other_query_ref, top_ref, other_top_ref, *refs):
    *fresh, _, _, sums_ref, other_sums_ref = refs
    own, other = shards_of([chip_ref], query_ref.shape[0])
    sets = [
        (own, query_ref, top_ref, sums_ref),
        (other, other_query_ref, other_top_ref, other_sums_ref),
    ]
    for ref in fresh:
        add_shards(sets, ref)


def repair(query_shard, near, refs, query_ref, top_ref, sums_ref):
    tokens = query_ref.shape[0]
    heads = query_ref.shape[1] // HEAD_DIM
    largest = functools.reduce(
        jnp.maximum, [sums_ref[head, :, HEAD_DIM:] for head in range(heads)]
    )

    @pl.when(jnp.logical_not(jnp.max(largest) < SAFE_SUM))
    def _():
        far = [(shard, None) for shard in shards_of(refs, tokens)]
        if near is not None:
            far = [(near, is_later())] + far

        def one_head(head, carried):
            query = query_ref[:, pl.ds(pl.multiple_of(head * HEAD_DIM, HEAD_DIM), HEAD_DIM)]
            for shard, usable in far:
                keys, _ = keys_and_values([shard], tokens)
                rows = penalties(query_shard, [shard], tokens, usable)
                scores = scaled_scores(query, keys)
                for query_block, row in enumerate(rows):
                    some = slice(query_block * BLK, (query_block + 1) * BLK)
                    top = top_ref[head, some]
                    for k, gap in enumerate(row):
                        seen = jnp.max(scores[some, columns(k)] - gap, axis=1, keepdims=True)
                        top = jnp.maximum(top, jnp.ceil(seen))
                    top_ref[head, some] = top
            top = top_ref[head]
            sums = jnp.zeros((tokens, 2 * HEAD_DIM), jnp.float32)
            if near is not None:
                keys, values = keys_and_values([query_shard], tokens)
                scores = scaled_scores(query, keys) + causal_bias(query_shard, tokens)
                weights = near_weights(scores, top, tokens)
                sums += jnp.dot(weights, values, preferred_element_type=jnp.float32)
            for shard, usable in far:
                keys, values = keys_and_values([shard], tokens)
                rows = penalties(query_shard, [shard], tokens, usable)
                weights = weights_of(scaled_scores(query, keys), top, rows)
                sums += jnp.dot(weights, values, preferred_element_type=jnp.float32)
            sums_ref[head] = sums
            return carried

        lax.fori_loop(0, heads, one_head, 0)


def side_lanes(top_ref, sums_ref, tokens):
    lane = lax.broadcasted_iota(jnp.int32, (tokens, HEAD_DIM), 1)
    heads = top_ref.shape[0]
    out = jnp.zeros((tokens, HEAD_DIM), jnp.float32)
    for head in range(heads):
        out = jnp.where(lane == head, sums_ref[head, :, HEAD_DIM:], out)
        out = jnp.where(lane == heads + head, top_ref[head], out)
    return out


def last_of_other(chip_ref, query_ref, top_in_ref, sums_in_ref, *refs):
    *fresh, out_ref, top_ref, sums_ref = refs
    tokens = query_ref.shape[0]
    heads = query_ref.shape[1] // HEAD_DIM
    _, other = shards_of([chip_ref], tokens)
    add_shards([(other, query_ref, top_ref, sums_ref)], fresh[-1])
    repair(other, None, fresh, query_ref, top_ref, sums_ref)
    for head in range(heads):
        out_ref[:, columns(head)] = sums_ref[head, :, :HEAD_DIM].astype(out_ref.dtype)
    side = side_lanes(top_ref, sums_ref, tokens)
    coarse = side.astype(out_ref.dtype)
    out_ref[:, columns(heads)] = coarse
    out_ref[:, columns(heads + 1)] = (side - coarse.astype(jnp.float32)).astype(out_ref.dtype)


def last_of_own(chip_ref, query_ref, top_in_ref, sums_in_ref, *refs):
    *fresh, top_ref, sums_ref = refs
    own, other = shards_of([chip_ref], query_ref.shape[0])
    add_shards([(own, query_ref, top_ref, sums_ref)], fresh[-1])
    repair(own, other, fresh, query_ref, top_ref, sums_ref)


def merge(top_ref, sums_ref, got_ref, out_ref, semaphores, ready):
    tokens = got_ref.shape[0]
    heads = top_ref.shape[0]
    side = got_ref[:, columns(heads)].astype(jnp.float32)
    side = side + got_ref[:, columns(heads + 1)].astype(jnp.float32)
    mine = side_lanes(top_ref, sums_ref, tokens)
    lane = lax.broadcasted_iota(jnp.int32, (tokens, HEAD_DIM), 1)
    apart = jnp.where((lane >= heads) & (lane < 2 * heads), jnp.abs(side - mine), 0.0)
    same = jnp.max(apart) == 0.0

    def spread(lane):
        return jnp.broadcast_to(side[:, lane : lane + 1], (tokens, HEAD_DIM))

    def divide(rescaled):
        for head in range(heads):
            mixture = sums_ref[head, :, :HEAD_DIM]
            row_sum = sums_ref[head, :, HEAD_DIM:]
            got = got_ref[:, columns(head)].astype(jnp.float32)
            got_sum = spread(head)
            if rescaled:
                top = top_ref[head]
                got_top = spread(heads + head)
                highest = jnp.maximum(top, got_top)
                here, there = jnp.exp2(top - highest), jnp.exp2(got_top - highest)
                mixture, row_sum = mixture * here, row_sum * here
                got, got_sum = got * there, got_sum * there
            ready[:, columns(head)] = ((mixture + got) / (row_sum + got_sum)).astype(ready.dtype)
            one_copy(head).start()

    def one_copy(head):
        at = columns(head)
        return pltpu.make_async_copy(ready.at[:, at], out_ref.at[:, at], semaphores.at[head])

    @pl.when(same)
    def _():
        divide(False)

    @pl.when(jnp.logical_not(same))
    def _():
        divide(True)

    for head in range(heads):
        one_copy(head).wait()


VMEM = pl.BlockSpec(memory_space=pltpu.VMEM)
HBM = pl.BlockSpec(memory_space=pltpu.HBM)


def in_vmem(*arrays):
    return [pltpu.with_memory_space_constraint(one, pltpu.VMEM) for one in arrays]


def call(body, out_shape, operands, aliases=None):
    return pl.pallas_call(
        body,
        out_shape=out_shape,
        in_specs=[VMEM] * len(operands),
        out_specs=jax.tree.map(lambda _: VMEM, out_shape),
        input_output_aliases=aliases or {},
        compiler_params=pltpu.CompilerParams(vmem_limit_bytes=40 << 20),
        cost_estimate=pl.CostEstimate(flops=1, bytes_accessed=1, transcendentals=0),
        name=body.__name__,
    )(*in_vmem(*operands))


def local(queries, keys, values, block_doc):
    tokens, width = queries.shape
    heads = width // HEAD_DIM
    inner_size = lax.axis_size("inner")
    count = lax.axis_size("outer") * inner_size
    assert count % PLANE == 0 and tokens % BLK == 0
    assert (DOC_BLOCKS - 1) * BLK <= 2 * PLANE * tokens
    position = lax.axis_index("outer") * inner_size + lax.axis_index("inner")
    place = position // PAIR % (PLANE // PAIR)
    later = position % PAIR == 1

    def send(array, target):
        route = [(d, target(d)) for d in range(count)]
        return lax.ppermute(array, AXES, [(a, b) for a, b in route if b is not None and b < count])

    def swapped(array):
        return send(array, lambda d: d ^ 1)

    def flipped(d, flip):
        return d ^ (PAIR * flip)

    payload = pl.pallas_call(
        pack,
        out_shape=pltpu.VMEM((shard_rows(tokens), HEAD_DIM), keys.dtype),
        in_specs=[HBM] * 3,
        out_specs=VMEM,
        scratch_shapes=[
            pltpu.SMEM(block_doc.shape, block_doc.dtype),
            pltpu.SemaphoreType.DMA((3,)),
        ],
        name="pack",
    )(block_doc, keys, values)
    chip = jnp.concatenate([payload, swapped(payload)], axis=0)
    other_queries = swapped(queries)

    def straight(d, flip):
        if d % PAIR == 0:
            return flipped(d, flip) + PLANE
        return flipped(d, flip) if flipped(d, flip) > d else flipped(d, flip) + 2 * PLANE if flip == 0 else None

    far = send(jnp.concatenate([chip, chip[:32]], axis=0), lambda d: straight(d, 0))
    ahead = send(chip, lambda d: straight(d, 3) if d % PAIR else None)
    across = send(chip, lambda d: None if d % PAIR else straight(d, 3))

    top_shape = pltpu.VMEM((heads, tokens, HEAD_DIM), jnp.float32)
    sums_shape = pltpu.VMEM((heads, tokens, 2 * HEAD_DIM), jnp.float32)
    top, other_top, sums, other_sums = call(
        first_stage,
        (top_shape, top_shape, sums_shape, sums_shape),
        (chip, queries, other_queries),
    )

    def add(sums, *fresh):
        operands = (chip, queries, other_queries, top, other_top, *fresh, *sums)
        at = len(operands) - 2
        return call(middle_stage, (sums_shape, sums_shape), operands, {at: 0, at + 1: 1})

    both = add((sums, other_sums), ahead)
    far, both = lax.optimization_barrier((far, both))
    far = far[: chip.shape[0]]

    def beside(step):
        before = place & jnp.where(later, 3 - step, step) == 0
        passed = jnp.where(later & before, chip, far)
        return send(passed, lambda d: flipped(d, 3 - step if d % PAIR else step))

    last = send(far, lambda d: flipped(d, 3) if d % PAIR and flipped(d, 3) < d else None)
    received = (ahead, far, across, beside(1), beside(2), last)
    for one in received[1:-2]:
        both = add(both, one)
    sums, other_sums = add(both, received[-2])
    message, _, _ = call(
        last_of_other,
        (pltpu.VMEM((tokens, width + 2 * HEAD_DIM), queries.dtype), top_shape, sums_shape),
        (chip, other_queries, other_top, other_sums, *received),
        {2: 1, 3: 2},
    )
    got = swapped(message)
    top, sums = call(
        last_of_own,
        (top_shape, sums_shape),
        (chip, queries, top, sums, *received),
        {2: 0, 3: 1},
    )
    return pl.pallas_call(
        merge,
        out_shape=jax.ShapeDtypeStruct(queries.shape, queries.dtype),
        in_specs=[VMEM] * 3,
        out_specs=HBM,
        scratch_shapes=[
            pltpu.SemaphoreType.DMA((heads,)),
            pltpu.VMEM(queries.shape, queries.dtype),
        ],
        compiler_params=pltpu.CompilerParams(vmem_limit_bytes=40 << 20),
        name="merge",
    )(*in_vmem(top, sums, got))


def solution(mesh):
    placed = (
        P(AXES, None),
        P(AXES, None),
        P(AXES, None),
        P(AXES),
    )
    return jax.shard_map(
        local, mesh=mesh, in_specs=placed, out_specs=P(AXES, None), check_vma=False
    )
```

```python
import functools
import math

import jax
import jax.numpy as jnp
from jax import lax
from jax.experimental import pallas as pl
from jax.experimental.pallas import tpu as pltpu
from jax.sharding import PartitionSpec as P

HEAD_DIM = 128
BLK = 128
DOC_BLOCKS = 32
AXES = ("outer", "inner")

PAIR = 2
PLANE = 8

MASKED = 1e30
SAFE_SUM = 2.0**100
TO_LOG2 = math.log2(math.e) / math.sqrt(HEAD_DIM)
DOC_ROWS = 8
ON_TRANSPOSED = (((1,), (1,)), ((), ()))


def shard_rows(tokens):
    return 2 * tokens + tokens // BLK * DOC_ROWS


def columns(head):
    return slice(head * HEAD_DIM, (head + 1) * HEAD_DIM)


def scaled_scores(query, key):
    return lax.dot_general(query, key, ON_TRANSPOSED, preferred_element_type=jnp.float32) * TO_LOG2


def shards_of(refs, tokens):
    rows = shard_rows(tokens)
    return [(ref, start) for ref in refs for start in range(0, ref.shape[0], rows)]


def keys_and_values(shards, tokens):
    keys = [ref[start : start + tokens] for ref, start in shards]
    values = [ref[start + tokens : start + 2 * tokens] for ref, start in shards]
    values = jnp.concatenate(values, axis=0)
    return jnp.concatenate(keys, axis=0), jnp.concatenate([values, jnp.ones_like(values)], axis=1)


def docs_of(shard, tokens):
    ref, start = shard
    at = [start + 2 * tokens + block * DOC_ROWS for block in range(tokens // BLK)]
    return [ref[k : k + DOC_ROWS].astype(jnp.float32)[:1] for k in at]


def penalties(query_shard, key_shards, tokens, usable=None):
    key_docs = [doc for shard in key_shards for doc in docs_of(shard, tokens)]
    rows = []
    for own in docs_of(query_shard, tokens):
        seen = [doc == own for doc in key_docs]
        if usable is not None:
            seen = [one & usable for one in seen]
        rows.append([jnp.where(one, 0.0, MASKED) for one in seen])
    return rows


def any_visible(rows):
    least = functools.reduce(jnp.minimum, [one for row in rows for one in row])
    return jnp.min(least) < 1.0


def weights_of(scores, top_ref, rows):
    out = []
    for query_block, row in enumerate(rows):
        at = slice(query_block * BLK, (query_block + 1) * BLK)
        top = top_ref[at]
        across = [
            jnp.exp2(scores[at, columns(k)] - (top + gap)).astype(jnp.bfloat16)
            for k, gap in enumerate(row)
        ]
        out.append(jnp.concatenate(across, axis=1))
    return jnp.concatenate(out, axis=0)


def causal_bias(shard, tokens):
    (docs,) = [docs_of(shard, tokens)]
    row = lax.broadcasted_iota(jnp.int32, (BLK, BLK), 0)
    column = lax.broadcasted_iota(jnp.int32, (BLK, BLK), 1)
    corner = jnp.where(column <= row, 0.0, -MASKED)
    out = []
    for query_block, own in enumerate(docs):
        across = []
        for block, doc in enumerate(docs):
            if block == query_block:
                across.append(corner)
            elif block < query_block:
                across.append(
                    jnp.broadcast_to(jnp.where(doc == own, 0.0, -MASKED), (BLK, BLK))
                )
            else:
                across.append(jnp.full((BLK, BLK), -MASKED, jnp.float32))
        out.append(jnp.concatenate(across, axis=1))
    return jnp.concatenate(out, axis=0)


def near_weights(scores, top, tokens):
    return jnp.concatenate(
        [
            jnp.exp2(scores[:, k : k + HEAD_DIM] - top).astype(jnp.bfloat16)
            for k in range(0, tokens, HEAD_DIM)
        ],
        axis=1,
    )


def is_later():
    position = lax.axis_index("outer") * lax.axis_size("inner") + lax.axis_index("inner")
    return position % PAIR == 1


def pack(doc_ref, keys_ref, values_ref, out_ref, doc_here, semaphores):
    tokens = keys_ref.shape[0]
    copies = [
        pltpu.make_async_copy(keys_ref, out_ref.at[:tokens], semaphores.at[0]),
        pltpu.make_async_copy(values_ref, out_ref.at[tokens : 2 * tokens], semaphores.at[1]),
        pltpu.make_async_copy(doc_ref, doc_here, semaphores.at[2]),
    ]
    for one in copies:
        one.start()
    copies[2].wait()
    shape = (tokens // BLK * DOC_ROWS, HEAD_DIM)
    block = lax.broadcasted_iota(jnp.int32, shape, 0) // DOC_ROWS
    docs = jnp.zeros(shape, jnp.int32)
    for k in range(tokens // BLK):
        docs = jnp.where(block == k, doc_here[k] + 1, docs)
    out_ref[2 * tokens :] = docs.astype(jnp.float32).astype(out_ref.dtype)
    copies[0].wait()
    copies[1].wait()


def first_stage(
    chip_ref, query_ref, other_query_ref, top_ref, other_top_ref, sums_ref, other_sums_ref
):
    tokens = query_ref.shape[0]
    own, other = shards_of([chip_ref], tokens)
    keys, values = keys_and_values([own, other], tokens)
    bias = causal_bias(own, tokens)
    other_bias = causal_bias(other, tokens)
    rows = penalties(own, [other], tokens, is_later())

    def reference(scores):
        top = jnp.ceil(jnp.max(scores, axis=1, keepdims=True))
        return jnp.broadcast_to(top, (tokens, HEAD_DIM))

    for head in range(query_ref.shape[1] // HEAD_DIM):
        scores = scaled_scores(query_ref[:, columns(head)], keys)
        near = scores[:, :tokens] + bias
        top = reference(near)
        top_ref[head] = top
        weights = [near_weights(near, top, tokens), weights_of(scores[:, tokens:], top, rows)]
        sums_ref[head] = jnp.dot(
            jnp.concatenate(weights, axis=1), values, preferred_element_type=jnp.float32
        )
        scores = scaled_scores(other_query_ref[:, columns(head)], keys[tokens:])
        other_top_ref[head] = reference(scores + other_bias)
    other_sums_ref[...] = jnp.zeros_like(other_sums_ref)


def add_shards(sets, ref):
    tokens = sets[0][1].shape[0]
    shards = shards_of([ref], tokens)
    gaps = [penalties(query_shard, shards, tokens) for query_shard, *_ in sets]
    seen = [any_visible(rows) for rows in gaps]

    def add(chosen):
        keys, values = keys_and_values(shards, tokens)
        for head in range(sets[0][1].shape[1] // HEAD_DIM):
            for k in chosen:
                _, query_ref, top_ref, sums_ref = sets[k]
                scores = scaled_scores(query_ref[:, columns(head)], keys)
                weights = weights_of(scores, top_ref.at[head], gaps[k])
                sums_ref[head] += jnp.dot(weights, values, preferred_element_type=jnp.float32)

    everything = range(len(sets))
    every = functools.reduce(jnp.logical_and, seen)
    pl.when(every)(lambda: add(everything))
    if len(sets) > 1:
        for k in everything:
            pl.when(seen[k] & jnp.logical_not(every))(lambda k=k: add([k]))


def middle_stage(chip_ref, query_ref, other_query_ref, top_ref, other_top_ref, *refs):
    *fresh, _, _, sums_ref, other_sums_ref = refs
    own, other = shards_of([chip_ref], query_ref.shape[0])
    sets = [
        (own, query_ref, top_ref, sums_ref),
        (other, other_query_ref, other_top_ref, other_sums_ref),
    ]
    for ref in fresh:
        add_shards(sets, ref)


def repair(query_shard, near, refs, query_ref, top_ref, sums_ref):
    tokens = query_ref.shape[0]
    heads = query_ref.shape[1] // HEAD_DIM
    largest = functools.reduce(
        jnp.maximum, [sums_ref[head, :, HEAD_DIM:] for head in range(heads)]
    )

    @pl.when(jnp.logical_not(jnp.max(largest) < SAFE_SUM))
    def _():
        far = [(shard, None) for shard in shards_of(refs, tokens)]
        if near is not None:
            far = [(near, is_later())] + far

        def one_head(head, carried):
            query = query_ref[:, pl.ds(pl.multiple_of(head * HEAD_DIM, HEAD_DIM), HEAD_DIM)]
            for shard, usable in far:
                keys, _ = keys_and_values([shard], tokens)
                rows = penalties(query_shard, [shard], tokens, usable)
                scores = scaled_scores(query, keys)
                for query_block, row in enumerate(rows):
                    some = slice(query_block * BLK, (query_block + 1) * BLK)
                    top = top_ref[head, some]
                    for k, gap in enumerate(row):
                        seen = jnp.max(scores[some, columns(k)] - gap, axis=1, keepdims=True)
                        top = jnp.maximum(top, jnp.ceil(seen))
                    top_ref[head, some] = top
            top = top_ref[head]
            sums = jnp.zeros((tokens, 2 * HEAD_DIM), jnp.float32)
            if near is not None:
                keys, values = keys_and_values([query_shard], tokens)
                scores = scaled_scores(query, keys) + causal_bias(query_shard, tokens)
                weights = near_weights(scores, top, tokens)
                sums += jnp.dot(weights, values, preferred_element_type=jnp.float32)
            for shard, usable in far:
                keys, values = keys_and_values([shard], tokens)
                rows = penalties(query_shard, [shard], tokens, usable)
                weights = weights_of(scaled_scores(query, keys), top, rows)
                sums += jnp.dot(weights, values, preferred_element_type=jnp.float32)
            sums_ref[head] = sums
            return carried

        lax.fori_loop(0, heads, one_head, 0)


def side_lanes(top_ref, sums_ref, tokens):
    lane = lax.broadcasted_iota(jnp.int32, (tokens, HEAD_DIM), 1)
    heads = top_ref.shape[0]
    out = jnp.zeros((tokens, HEAD_DIM), jnp.float32)
    for head in range(heads):
        out = jnp.where(lane == head, sums_ref[head, :, HEAD_DIM:], out)
        out = jnp.where(lane == heads + head, top_ref[head], out)
    return out


def last_of_other(chip_ref, query_ref, top_in_ref, sums_in_ref, *refs):
    *fresh, out_ref, top_ref, sums_ref = refs
    tokens = query_ref.shape[0]
    heads = query_ref.shape[1] // HEAD_DIM
    _, other = shards_of([chip_ref], tokens)
    add_shards([(other, query_ref, top_ref, sums_ref)], fresh[-1])
    repair(other, None, fresh, query_ref, top_ref, sums_ref)
    for head in range(heads):
        out_ref[:, columns(head)] = sums_ref[head, :, :HEAD_DIM].astype(out_ref.dtype)
    side = side_lanes(top_ref, sums_ref, tokens)
    coarse = side.astype(out_ref.dtype)
    out_ref[:, columns(heads)] = coarse
    out_ref[:, columns(heads + 1)] = (side - coarse.astype(jnp.float32)).astype(out_ref.dtype)


def last_of_own(chip_ref, query_ref, top_in_ref, sums_in_ref, *refs):
    *fresh, top_ref, sums_ref = refs
    own, other = shards_of([chip_ref], query_ref.shape[0])
    add_shards([(own, query_ref, top_ref, sums_ref)], fresh[-1])
    repair(own, other, fresh, query_ref, top_ref, sums_ref)


def merge(top_ref, sums_ref, got_ref, out_ref, semaphores, ready):
    tokens = got_ref.shape[0]
    heads = top_ref.shape[0]
    side = got_ref[:, columns(heads)].astype(jnp.float32)
    side = side + got_ref[:, columns(heads + 1)].astype(jnp.float32)
    mine = side_lanes(top_ref, sums_ref, tokens)
    lane = lax.broadcasted_iota(jnp.int32, (tokens, HEAD_DIM), 1)
    apart = jnp.where((lane >= heads) & (lane < 2 * heads), jnp.abs(side - mine), 0.0)
    same = jnp.max(apart) == 0.0

    def spread(lane):
        return jnp.broadcast_to(side[:, lane : lane + 1], (tokens, HEAD_DIM))

    def divide(rescaled):
        for head in range(heads):
            mixture = sums_ref[head, :, :HEAD_DIM]
            row_sum = sums_ref[head, :, HEAD_DIM:]
            got = got_ref[:, columns(head)].astype(jnp.float32)
            got_sum = spread(head)
            if rescaled:
                top = top_ref[head]
                got_top = spread(heads + head)
                highest = jnp.maximum(top, got_top)
                here, there = jnp.exp2(top - highest), jnp.exp2(got_top - highest)
                mixture, row_sum = mixture * here, row_sum * here
                got, got_sum = got * there, got_sum * there
            ready[:, columns(head)] = ((mixture + got) / (row_sum + got_sum)).astype(ready.dtype)
            one_copy(head).start()

    def one_copy(head):
        at = columns(head)
        return pltpu.make_async_copy(ready.at[:, at], out_ref.at[:, at], semaphores.at[head])

    @pl.when(same)
    def _():
        divide(False)

    @pl.when(jnp.logical_not(same))
    def _():
        divide(True)

    for head in range(heads):
        one_copy(head).wait()


VMEM = pl.BlockSpec(memory_space=pltpu.VMEM)
HBM = pl.BlockSpec(memory_space=pltpu.HBM)


def in_vmem(*arrays):
    return [pltpu.with_memory_space_constraint(one, pltpu.VMEM) for one in arrays]


def call(body, out_shape, operands, aliases=None):
    return pl.pallas_call(
        body,
        out_shape=out_shape,
        in_specs=[VMEM] * len(operands),
        out_specs=jax.tree.map(lambda _: VMEM, out_shape),
        input_output_aliases=aliases or {},
        compiler_params=pltpu.CompilerParams(vmem_limit_bytes=40 << 20),
        cost_estimate=pl.CostEstimate(flops=1, bytes_accessed=1, transcendentals=0),
        name=body.__name__,
    )(*in_vmem(*operands))


def local(queries, keys, values, block_doc):
    tokens, width = queries.shape
    heads = width // HEAD_DIM
    inner_size = lax.axis_size("inner")
    count = lax.axis_size("outer") * inner_size
    assert count % PLANE == 0 and tokens % BLK == 0
    assert (DOC_BLOCKS - 1) * BLK <= 2 * PLANE * tokens
    position = lax.axis_index("outer") * inner_size + lax.axis_index("inner")
    place = position // PAIR % (PLANE // PAIR)
    later = position % PAIR == 1

    def send(array, target):
        route = [(d, target(d)) for d in range(count)]
        return lax.ppermute(array, AXES, [(a, b) for a, b in route if b is not None and b < count])

    def swapped(array):
        return send(array, lambda d: d ^ 1)

    def flipped(d, flip):
        return d ^ (PAIR * flip)

    payload = pl.pallas_call(
        pack,
        out_shape=pltpu.VMEM((shard_rows(tokens), HEAD_DIM), keys.dtype),
        in_specs=[HBM] * 3,
        out_specs=VMEM,
        scratch_shapes=[
            pltpu.SMEM(block_doc.shape, block_doc.dtype),
            pltpu.SemaphoreType.DMA((3,)),
        ],
        name="pack",
    )(block_doc, keys, values)
    chip = jnp.concatenate([payload, swapped(payload)], axis=0)
    other_queries = swapped(queries)

    def straight(d, flip):
        if d % PAIR == 0:
            return flipped(d, flip) + PLANE
        return flipped(d, flip) if flipped(d, flip) > d else flipped(d, flip) + 2 * PLANE if flip == 0 else None

    far = send(chip, lambda d: straight(d, 0))
    across = send(chip, lambda d: straight(d, 3))

    top_shape = pltpu.VMEM((heads, tokens, HEAD_DIM), jnp.float32)
    sums_shape = pltpu.VMEM((heads, tokens, 2 * HEAD_DIM), jnp.float32)
    top, other_top, sums, other_sums = call(
        first_stage,
        (top_shape, top_shape, sums_shape, sums_shape),
        (chip, queries, other_queries),
    )

    def add(sums, *fresh):
        operands = (chip, queries, other_queries, top, other_top, *fresh, *sums)
        at = len(operands) - 2
        return call(middle_stage, (sums_shape, sums_shape), operands, {at: 0, at + 1: 1})

    far, both = lax.optimization_barrier((far, (sums, other_sums)))

    def beside(step):
        before = place & jnp.where(later, 3 - step, step) == 0
        passed = jnp.where(later & before, chip, far)
        return send(passed, lambda d: flipped(d, 3 - step if d % PAIR else step))

    last = send(far, lambda d: flipped(d, 3) if d % PAIR and flipped(d, 3) < d else None)
    received = (far, across, beside(1), beside(2), last)
    for one in received[:-2]:
        both = add(both, one)
    sums, other_sums = add(both, received[-2])
    message, _, _ = call(
        last_of_other,
        (pltpu.VMEM((tokens, width + 2 * HEAD_DIM), queries.dtype), top_shape, sums_shape),
        (chip, other_queries, other_top, other_sums, *received),
        {2: 1, 3: 2},
    )
    got = swapped(message)
    top, sums = call(
        last_of_own,
        (top_shape, sums_shape),
        (chip, queries, top, sums, *received),
        {2: 0, 3: 1},
    )
    return pl.pallas_call(
        merge,
        out_shape=jax.ShapeDtypeStruct(queries.shape, queries.dtype),
        in_specs=[VMEM] * 3,
        out_specs=HBM,
        scratch_shapes=[
            pltpu.SemaphoreType.DMA((heads,)),
            pltpu.VMEM(queries.shape, queries.dtype),
        ],
        compiler_params=pltpu.CompilerParams(vmem_limit_bytes=40 << 20),
        name="merge",
    )(*in_vmem(top, sums, got))


def solution(mesh):
    placed = (
        P(AXES, None),
        P(AXES, None),
        P(AXES, None),
        P(AXES),
    )
    return jax.shard_map(
        local, mesh=mesh, in_specs=placed, out_specs=P(AXES, None), check_vma=False
    )
```

```python
import functools
import math

import jax
import jax.numpy as jnp
from jax import lax
from jax.experimental import pallas as pl
from jax.experimental.pallas import tpu as pltpu
from jax.sharding import PartitionSpec as P

HEAD_DIM = 128
BLK = 128
DOC_BLOCKS = 32
AXES = ("outer", "inner")

PAIR = 2
PLANE = 8

MASKED = 1e30
SAFE_SUM = 2.0**100
TO_LOG2 = math.log2(math.e) / math.sqrt(HEAD_DIM)
DOC_ROWS = 8
ON_TRANSPOSED = (((1,), (1,)), ((), ()))


def shard_rows(tokens):
    return 2 * tokens + tokens // BLK * DOC_ROWS


def columns(head):
    return slice(head * HEAD_DIM, (head + 1) * HEAD_DIM)


def scaled_scores(query, key):
    return lax.dot_general(query, key, ON_TRANSPOSED, preferred_element_type=jnp.float32) * TO_LOG2


def shards_of(refs, tokens):
    rows = shard_rows(tokens)
    return [(ref, start) for ref in refs for start in range(0, ref.shape[0], rows)]


def keys_and_values(shards, tokens):
    keys = [ref[start : start + tokens] for ref, start in shards]
    values = [ref[start + tokens : start + 2 * tokens] for ref, start in shards]
    values = jnp.concatenate(values, axis=0)
    return jnp.concatenate(keys, axis=0), jnp.concatenate([values, jnp.ones_like(values)], axis=1)


def docs_of(shard, tokens):
    ref, start = shard
    docs = ref[start + 2 * tokens : start + shard_rows(tokens)].astype(jnp.float32)
    return [docs[k : k + 1] for k in range(0, tokens // BLK * DOC_ROWS, DOC_ROWS)]


def penalties(query_shard, key_shards, tokens, usable=None):
    key_docs = [doc for shard in key_shards for doc in docs_of(shard, tokens)]
    rows = []
    for own in docs_of(query_shard, tokens):
        seen = [doc == own for doc in key_docs]
        if usable is not None:
            seen = [one & usable for one in seen]
        rows.append([jnp.where(one, 0.0, MASKED) for one in seen])
    return rows


def any_visible(rows):
    least = functools.reduce(jnp.minimum, [one for row in rows for one in row])
    return jnp.min(least) < 1.0


def weights_of(scores, top_ref, rows):
    out = []
    for query_block, row in enumerate(rows):
        at = slice(query_block * BLK, (query_block + 1) * BLK)
        top = top_ref[at]
        across = [
            jnp.exp2(scores[at, columns(k)] - (top + gap)).astype(jnp.bfloat16)
            for k, gap in enumerate(row)
        ]
        out.append(jnp.concatenate(across, axis=1))
    return jnp.concatenate(out, axis=0)


def causal_bias(shard, tokens):
    docs = docs_of(shard, tokens)
    row = lax.broadcasted_iota(jnp.int32, (BLK, BLK), 0)
    column = lax.broadcasted_iota(jnp.int32, (BLK, BLK), 1)
    corner = jnp.where(column <= row, 0.0, -MASKED)
    out = []
    for query_block, own in enumerate(docs):
        across = []
        for block, doc in enumerate(docs):
            if block == query_block:
                across.append(corner)
            elif block < query_block:
                across.append(
                    jnp.broadcast_to(jnp.where(doc == own, 0.0, -MASKED), (BLK, BLK))
                )
            else:
                across.append(jnp.full((BLK, BLK), -MASKED, jnp.float32))
        out.append(jnp.concatenate(across, axis=1))
    return jnp.concatenate(out, axis=0)


def near_weights(scores, top, tokens):
    return jnp.concatenate(
        [
            jnp.exp2(scores[:, k : k + HEAD_DIM] - top).astype(jnp.bfloat16)
            for k in range(0, tokens, HEAD_DIM)
        ],
        axis=1,
    )


def own_position():
    return lax.axis_index("outer") * lax.axis_size("inner") + lax.axis_index("inner")


def is_later():
    return own_position() % PAIR == 1


def gets_last():
    return is_later() & (own_position() % PLANE < PLANE // 2)


def pack(doc_ref, keys_ref, values_ref, out_ref, doc_here, semaphores):
    tokens = keys_ref.shape[0]
    copies = [
        pltpu.make_async_copy(keys_ref, out_ref.at[:tokens], semaphores.at[0]),
        pltpu.make_async_copy(values_ref, out_ref.at[tokens : 2 * tokens], semaphores.at[1]),
        pltpu.make_async_copy(doc_ref, doc_here, semaphores.at[2]),
    ]
    for one in copies:
        one.start()
    copies[2].wait()
    shape = (tokens // BLK * DOC_ROWS, HEAD_DIM)
    block = lax.broadcasted_iota(jnp.int32, shape, 0) // DOC_ROWS
    docs = jnp.zeros(shape, jnp.int32)
    for k in range(tokens // BLK):
        docs = jnp.where(block == k, doc_here[k] + 1, docs)
    out_ref[2 * tokens :] = docs.astype(jnp.float32).astype(out_ref.dtype)
    copies[0].wait()
    copies[1].wait()


def first_stage(
    chip_ref, query_ref, other_query_ref, top_ref, other_top_ref, sums_ref, other_sums_ref
):
    tokens = query_ref.shape[0]
    own, other = shards_of([chip_ref], tokens)
    keys, values = keys_and_values([own, other], tokens)
    bias = causal_bias(own, tokens)
    other_bias = causal_bias(other, tokens)
    rows = penalties(own, [other], tokens, is_later())

    def reference(scores):
        top = jnp.ceil(jnp.max(scores, axis=1, keepdims=True))
        return jnp.broadcast_to(top, (tokens, HEAD_DIM))

    for head in range(query_ref.shape[1] // HEAD_DIM):
        scores = scaled_scores(query_ref[:, columns(head)], keys)
        near = scores[:, :tokens] + bias
        top = reference(near)
        top_ref[head] = top
        weights = [near_weights(near, top, tokens), weights_of(scores[:, tokens:], top, rows)]
        sums_ref[head] = jnp.dot(
            jnp.concatenate(weights, axis=1), values, preferred_element_type=jnp.float32
        )
        scores = scaled_scores(other_query_ref[:, columns(head)], keys[tokens:])
        other_top_ref[head] = reference(scores + other_bias)
    other_sums_ref[...] = jnp.zeros_like(other_sums_ref)


def add_shards(sets, ref, wanted=None):
    tokens = sets[0][1].shape[0]
    shards = shards_of([ref], tokens)
    gaps = [penalties(query_shard, shards, tokens) for query_shard, *_ in sets]
    seen = [any_visible(rows) for rows in gaps]
    if wanted is not None:
        seen = [one & wanted for one in seen]

    def add(chosen):
        keys, values = keys_and_values(shards, tokens)
        for head in range(sets[0][1].shape[1] // HEAD_DIM):
            for k in chosen:
                _, query_ref, top_ref, sums_ref = sets[k]
                scores = scaled_scores(query_ref[:, columns(head)], keys)
                weights = weights_of(scores, top_ref.at[head], gaps[k])
                sums_ref[head] += jnp.dot(weights, values, preferred_element_type=jnp.float32)

    everything = range(len(sets))
    every = functools.reduce(jnp.logical_and, seen)
    pl.when(every)(lambda: add(everything))
    if len(sets) > 1:
        for k in everything:
            pl.when(seen[k] & jnp.logical_not(every))(lambda k=k: add([k]))


def middle_stage(chip_ref, query_ref, other_query_ref, top_ref, other_top_ref, *refs):
    *fresh, _, _, sums_ref, other_sums_ref = refs
    own, other = shards_of([chip_ref], query_ref.shape[0])
    sets = [
        (own, query_ref, top_ref, sums_ref),
        (other, other_query_ref, other_top_ref, other_sums_ref),
    ]
    for ref in fresh:
        add_shards(sets, ref)


def late_stage(chip_ref, query_ref, other_query_ref, top_ref, other_top_ref, *refs):
    ref, _, _, sums_ref, other_sums_ref = refs
    own, other = shards_of([chip_ref], query_ref.shape[0])
    sets = [
        (own, query_ref, top_ref, sums_ref),
        (other, other_query_ref, other_top_ref, other_sums_ref),
    ]
    add_shards(sets, ref, gets_last())


def repair(query_shard, near, refs, query_ref, top_ref, sums_ref, then=None):
    tokens = query_ref.shape[0]
    heads = query_ref.shape[1] // HEAD_DIM
    largest = functools.reduce(
        jnp.maximum, [sums_ref[head, :, HEAD_DIM:] for head in range(heads)]
    )

    @pl.when(jnp.logical_not(jnp.max(largest) < SAFE_SUM))
    def _():
        far = [(shard, None) for shard in shards_of(refs, tokens)]
        if near is not None:
            far = [(near, is_later())] + far

        def one_head(head, carried):
            query = query_ref[:, pl.ds(pl.multiple_of(head * HEAD_DIM, HEAD_DIM), HEAD_DIM)]
            for shard, usable in far:
                keys, _ = keys_and_values([shard], tokens)
                rows = penalties(query_shard, [shard], tokens, usable)
                scores = scaled_scores(query, keys)
                for query_block, row in enumerate(rows):
                    some = slice(query_block * BLK, (query_block + 1) * BLK)
                    top = top_ref[head, some]
                    for k, gap in enumerate(row):
                        seen = jnp.max(scores[some, columns(k)] - gap, axis=1, keepdims=True)
                        top = jnp.maximum(top, jnp.ceil(seen))
                    top_ref[head, some] = top
            top = top_ref[head]
            sums = jnp.zeros((tokens, 2 * HEAD_DIM), jnp.float32)
            if near is not None:
                keys, values = keys_and_values([query_shard], tokens)
                scores = scaled_scores(query, keys) + causal_bias(query_shard, tokens)
                weights = near_weights(scores, top, tokens)
                sums += jnp.dot(weights, values, preferred_element_type=jnp.float32)
            for shard, usable in far:
                keys, values = keys_and_values([shard], tokens)
                rows = penalties(query_shard, [shard], tokens, usable)
                weights = weights_of(scaled_scores(query, keys), top, rows)
                sums += jnp.dot(weights, values, preferred_element_type=jnp.float32)
            sums_ref[head] = sums
            return carried

        lax.fori_loop(0, heads, one_head, 0)
        if then is not None:
            then()


def side_lanes(top_ref, sums_ref, tokens):
    lane = lax.broadcasted_iota(jnp.int32, (tokens, HEAD_DIM), 1)
    heads = top_ref.shape[0]
    out = jnp.zeros((tokens, HEAD_DIM), jnp.float32)
    for head in range(heads):
        out = jnp.where(lane == head, sums_ref[head, :, HEAD_DIM:], out)
        out = jnp.where(lane == heads + head, top_ref[head], out)
    return out


def last_of_other(chip_ref, query_ref, top_in_ref, sums_in_ref, *refs):
    *fresh, out_ref, top_ref, sums_ref = refs
    tokens = query_ref.shape[0]
    heads = query_ref.shape[1] // HEAD_DIM
    _, other = shards_of([chip_ref], tokens)
    sets = [(other, query_ref, top_ref, sums_ref)]
    add_shards(sets, fresh[-2], jnp.logical_not(gets_last()))
    add_shards(sets, fresh[-1])

    def write():
        for head in range(heads):
            out_ref[:, columns(head)] = sums_ref[head, :, :HEAD_DIM].astype(out_ref.dtype)
        side = side_lanes(top_ref, sums_ref, tokens)
        coarse = side.astype(out_ref.dtype)
        out_ref[:, columns(heads)] = coarse
        out_ref[:, columns(heads + 1)] = (side - coarse.astype(jnp.float32)).astype(out_ref.dtype)

    write()
    repair(other, None, fresh, query_ref, top_ref, sums_ref, write)


def last_of_own(chip_ref, query_ref, top_in_ref, sums_in_ref, *refs):
    *fresh, top_ref, sums_ref = refs
    own, other = shards_of([chip_ref], query_ref.shape[0])
    sets = [(own, query_ref, top_ref, sums_ref)]
    add_shards(sets, fresh[-2], jnp.logical_not(gets_last()))
    add_shards(sets, fresh[-1])
    repair(own, other, fresh, query_ref, top_ref, sums_ref)


def merge(top_ref, sums_ref, got_ref, out_ref, semaphores, ready):
    tokens = got_ref.shape[0]
    heads = top_ref.shape[0]
    side = got_ref[:, columns(heads)].astype(jnp.float32)
    side = side + got_ref[:, columns(heads + 1)].astype(jnp.float32)
    mine = side_lanes(top_ref, sums_ref, tokens)
    lane = lax.broadcasted_iota(jnp.int32, (tokens, HEAD_DIM), 1)
    apart = jnp.where((lane >= heads) & (lane < 2 * heads), jnp.abs(side - mine), 0.0)
    same = jnp.max(apart) == 0.0

    def spread(lane):
        return jnp.broadcast_to(side[:, lane : lane + 1], (tokens, HEAD_DIM))

    def divide(rescaled):
        for head in range(heads):
            mixture = sums_ref[head, :, :HEAD_DIM]
            row_sum = sums_ref[head, :, HEAD_DIM:]
            got = got_ref[:, columns(head)].astype(jnp.float32)
            got_sum = spread(head)
            if rescaled:
                top = top_ref[head]
                got_top = spread(heads + head)
                highest = jnp.maximum(top, got_top)
                here, there = jnp.exp2(top - highest), jnp.exp2(got_top - highest)
                mixture, row_sum = mixture * here, row_sum * here
                got, got_sum = got * there, got_sum * there
            ready[:, columns(head)] = ((mixture + got) / (row_sum + got_sum)).astype(ready.dtype)
            one_copy(head).start()

    def one_copy(head):
        at = columns(head)
        return pltpu.make_async_copy(ready.at[:, at], out_ref.at[:, at], semaphores.at[head])

    def wait():
        for head in range(heads):
            one_copy(head).wait()

    divide(False)
    wait()

    @pl.when(jnp.logical_not(same))
    def _():
        divide(True)
        wait()


VMEM = pl.BlockSpec(memory_space=pltpu.VMEM)
HBM = pl.BlockSpec(memory_space=pltpu.HBM)


def in_vmem(*arrays):
    return [pltpu.with_memory_space_constraint(one, pltpu.VMEM) for one in arrays]


def call(body, out_shape, operands, aliases=None):
    return pl.pallas_call(
        body,
        out_shape=out_shape,
        in_specs=[VMEM] * len(operands),
        out_specs=jax.tree.map(lambda _: VMEM, out_shape),
        input_output_aliases=aliases or {},
        compiler_params=pltpu.CompilerParams(vmem_limit_bytes=40 << 20),
        cost_estimate=pl.CostEstimate(flops=1, bytes_accessed=1, transcendentals=0),
        name=body.__name__,
    )(*in_vmem(*operands))


def local(queries, keys, values, block_doc):
    tokens, width = queries.shape
    heads = width // HEAD_DIM
    inner_size = lax.axis_size("inner")
    count = lax.axis_size("outer") * inner_size
    assert count % PLANE == 0 and tokens % BLK == 0
    assert (DOC_BLOCKS - 1) * BLK <= 2 * PLANE * tokens
    position = lax.axis_index("outer") * inner_size + lax.axis_index("inner")
    place = position // PAIR % (PLANE // PAIR)
    later = position % PAIR == 1

    def send(array, target):
        route = [(d, target(d)) for d in range(count)]
        return lax.ppermute(array, AXES, [(a, b) for a, b in route if b is not None and b < count])

    def swapped(array):
        return send(array, lambda d: d ^ 1)

    def flipped(d, flip):
        return d ^ (PAIR * flip)

    payload = pl.pallas_call(
        pack,
        out_shape=pltpu.VMEM((shard_rows(tokens), HEAD_DIM), keys.dtype),
        in_specs=[HBM] * 3,
        out_specs=VMEM,
        scratch_shapes=[
            pltpu.SMEM(block_doc.shape, block_doc.dtype),
            pltpu.SemaphoreType.DMA((3,)),
        ],
        name="pack",
    )(block_doc, keys, values)
    chip = jnp.concatenate([payload, swapped(payload)], axis=0)
    other_queries = swapped(queries)

    def straight(d, flip):
        if d % PAIR == 0:
            return flipped(d, flip) + PLANE
        return flipped(d, flip) if flipped(d, flip) > d else flipped(d, flip) + 2 * PLANE if flip == 0 else None

    far = send(chip, lambda d: straight(d, 0))
    across = send(chip, lambda d: straight(d, 3))

    top_shape = pltpu.VMEM((heads, tokens, HEAD_DIM), jnp.float32)
    sums_shape = pltpu.VMEM((heads, tokens, 2 * HEAD_DIM), jnp.float32)
    top, other_top, sums, other_sums = call(
        first_stage,
        (top_shape, top_shape, sums_shape, sums_shape),
        (chip, queries, other_queries),
    )

    def add(sums, *fresh, stage=middle_stage):
        operands = (chip, queries, other_queries, top, other_top, *fresh, *sums)
        at = len(operands) - 2
        return call(stage, (sums_shape, sums_shape), operands, {at: 0, at + 1: 1})

    far, both = lax.optimization_barrier((far, (sums, other_sums)))

    def beside(step):
        before = place & jnp.where(later, 3 - step, step) == 0
        passed = jnp.where(later & before, chip, far)
        return send(passed, lambda d: flipped(d, 3 - step if d % PAIR else step))

    last = send(far, lambda d: flipped(d, 3) if d % PAIR and flipped(d, 3) < d else None)
    received = (far, across, beside(1), beside(2), last)
    for one in received[:-2]:
        both = add(both, one)
    sums, other_sums = add(both, received[-2], stage=late_stage)
    message, _, _ = call(
        last_of_other,
        (pltpu.VMEM((tokens, width + 2 * HEAD_DIM), queries.dtype), top_shape, sums_shape),
        (chip, other_queries, other_top, other_sums, *received),
        {2: 1, 3: 2},
    )
    got = swapped(message)
    top, sums = call(
        last_of_own,
        (top_shape, sums_shape),
        (chip, queries, top, sums, *received),
        {2: 0, 3: 1},
    )
    return pl.pallas_call(
        merge,
        out_shape=jax.ShapeDtypeStruct(queries.shape, queries.dtype),
        in_specs=[VMEM] * 3,
        out_specs=HBM,
        scratch_shapes=[
            pltpu.SemaphoreType.DMA((heads,)),
            pltpu.VMEM(queries.shape, queries.dtype),
        ],
        compiler_params=pltpu.CompilerParams(vmem_limit_bytes=40 << 20),
        name="merge",
    )(*in_vmem(top, sums, got))


def solution(mesh):
    placed = (
        P(AXES, None),
        P(AXES, None),
        P(AXES, None),
        P(AXES),
    )
    return jax.shard_map(
        local, mesh=mesh, in_specs=placed, out_specs=P(AXES, None), check_vma=False
    )
```

```python
import functools
import math

import jax
import jax.numpy as jnp
from jax import lax
from jax.experimental import pallas as pl
from jax.experimental.pallas import tpu as pltpu
from jax.sharding import PartitionSpec as P

HEAD_DIM = 128
BLK = 128
DOC_BLOCKS = 32
AXES = ("outer", "inner")

PAIR = 2
PLANE = 8

MASKED = 1e30
SAFE_SUM = 2.0**100
TO_LOG2 = math.log2(math.e) / math.sqrt(HEAD_DIM)
HALF = HEAD_DIM // 2
DOC_ROWS = 8
ON_TRANSPOSED = (((1,), (1,)), ((), ()))


def shard_rows(tokens):
    return 2 * tokens + tokens // BLK * DOC_ROWS


def columns(head):
    return slice(head * HEAD_DIM, (head + 1) * HEAD_DIM)


def scaled_scores(query, key):
    return lax.dot_general(query, key, ON_TRANSPOSED, preferred_element_type=jnp.float32) * TO_LOG2


def shards_of(refs, tokens):
    rows = shard_rows(tokens)
    return [(ref, start) for ref in refs for start in range(0, ref.shape[0], rows)]


def keys_and_values(shards, tokens):
    keys = [ref[start : start + tokens] for ref, start in shards]
    values = [ref[start + tokens : start + 2 * tokens] for ref, start in shards]
    values = jnp.concatenate(values, axis=0)
    return jnp.concatenate(keys, axis=0), jnp.concatenate([values, jnp.ones_like(values)], axis=1)


def docs_of(shard, tokens):
    ref, start = shard
    docs = ref[start + 2 * tokens : start + shard_rows(tokens)].astype(jnp.float32)
    return [docs[k : k + 1] for k in range(0, tokens // BLK * DOC_ROWS, DOC_ROWS)]


def penalties(query_shard, key_shards, tokens, usable=None):
    key_docs = [doc for shard in key_shards for doc in docs_of(shard, tokens)]
    rows = []
    for own in docs_of(query_shard, tokens):
        seen = [doc == own for doc in key_docs]
        if usable is not None:
            seen = [one & usable for one in seen]
        rows.append([jnp.where(one, 0.0, MASKED) for one in seen])
    return rows


def any_visible(rows):
    least = functools.reduce(jnp.minimum, [one for row in rows for one in row])
    return jnp.min(least) < 1.0


def weights_of(scores, top_ref, rows):
    out = []
    for query_block, row in enumerate(rows):
        at = slice(query_block * BLK, (query_block + 1) * BLK)
        top = top_ref[at]
        across = [
            jnp.exp2(scores[at, columns(k)] - (top + gap)).astype(jnp.bfloat16)
            for k, gap in enumerate(row)
        ]
        out.append(jnp.concatenate(across, axis=1))
    return jnp.concatenate(out, axis=0)


def causal_bias(shard, tokens):
    docs = docs_of(shard, tokens)
    row = lax.broadcasted_iota(jnp.int32, (BLK, BLK), 0)
    column = lax.broadcasted_iota(jnp.int32, (BLK, BLK), 1)
    corner = jnp.where(column <= row, 0.0, -MASKED)
    out = []
    for query_block, own in enumerate(docs):
        across = []
        for block, doc in enumerate(docs):
            if block == query_block:
                across.append(corner)
            elif block < query_block:
                across.append(
                    jnp.broadcast_to(jnp.where(doc == own, 0.0, -MASKED), (BLK, BLK))
                )
            else:
                across.append(jnp.full((BLK, BLK), -MASKED, jnp.float32))
        out.append(jnp.concatenate(across, axis=1))
    return jnp.concatenate(out, axis=0)


def near_weights(scores, top, tokens):
    return jnp.concatenate(
        [
            jnp.exp2(scores[:, k : k + HEAD_DIM] - top).astype(jnp.bfloat16)
            for k in range(0, tokens, HEAD_DIM)
        ],
        axis=1,
    )


def own_position():
    return lax.axis_index("outer") * lax.axis_size("inner") + lax.axis_index("inner")


def is_later():
    return own_position() % PAIR == 1


def gets_last():
    return is_later() & (own_position() % PLANE < PLANE // 2)


def pack(doc_ref, keys_ref, values_ref, out_ref, doc_here, semaphores):
    tokens = keys_ref.shape[0]
    copies = [
        pltpu.make_async_copy(keys_ref, out_ref.at[:tokens], semaphores.at[0]),
        pltpu.make_async_copy(values_ref, out_ref.at[tokens : 2 * tokens], semaphores.at[1]),
        pltpu.make_async_copy(doc_ref, doc_here, semaphores.at[2]),
    ]
    for one in copies:
        one.start()
    copies[2].wait()
    shape = (tokens // BLK * DOC_ROWS, HEAD_DIM)
    block = lax.broadcasted_iota(jnp.int32, shape, 0) // DOC_ROWS
    docs = jnp.zeros(shape, jnp.int32)
    for k in range(tokens // BLK):
        docs = jnp.where(block == k, doc_here[k] + 1, docs)
    out_ref[2 * tokens :] = docs.astype(jnp.float32).astype(out_ref.dtype)
    copies[0].wait()
    copies[1].wait()


def first_stage(
    chip_ref, query_ref, other_query_ref, top_ref, other_top_ref, sums_ref, other_sums_ref
):
    tokens = query_ref.shape[0]
    own, other = shards_of([chip_ref], tokens)
    keys, values = keys_and_values([own, other], tokens)
    bias = causal_bias(own, tokens)
    other_bias = causal_bias(other, tokens)
    rows = penalties(own, [other], tokens, is_later())

    def reference(scores):
        top = jnp.ceil(jnp.max(scores, axis=1, keepdims=True))
        return jnp.broadcast_to(top, (tokens, HEAD_DIM))

    for head in range(query_ref.shape[1] // HEAD_DIM):
        scores = scaled_scores(query_ref[:, columns(head)], keys)
        near = scores[:, :tokens] + bias
        top = reference(near)
        top_ref[head] = top
        weights = [near_weights(near, top, tokens), weights_of(scores[:, tokens:], top, rows)]
        sums_ref[head] = jnp.dot(
            jnp.concatenate(weights, axis=1), values, preferred_element_type=jnp.float32
        )
        scores = scaled_scores(other_query_ref[:, columns(head)], keys[tokens:])
        other_top_ref[head] = reference(scores + other_bias)
    other_sums_ref[...] = jnp.zeros_like(other_sums_ref)


def add_shards(sets, ref, wanted=None):
    tokens = sets[0][1].shape[0]
    shards = shards_of([ref], tokens)
    gaps = [penalties(query_shard, shards, tokens) for query_shard, *_ in sets]
    seen = [any_visible(rows) for rows in gaps]
    if wanted is not None:
        seen = [one & wanted for one in seen]

    def add(chosen):
        keys, values = keys_and_values(shards, tokens)
        for head in range(sets[0][1].shape[1] // HEAD_DIM):
            for k in chosen:
                _, query_ref, top_ref, sums_ref = sets[k]
                scores = scaled_scores(query_ref[:, columns(head)], keys)
                weights = weights_of(scores, top_ref.at[head], gaps[k])
                sums_ref[head] += jnp.dot(weights, values, preferred_element_type=jnp.float32)

    everything = range(len(sets))
    every = functools.reduce(jnp.logical_and, seen)
    pl.when(every)(lambda: add(everything))
    if len(sets) > 1:
        for k in everything:
            pl.when(seen[k] & jnp.logical_not(every))(lambda k=k: add([k]))


def middle_stage(chip_ref, query_ref, other_query_ref, top_ref, other_top_ref, *refs):
    *fresh, _, _, sums_ref, other_sums_ref = refs
    own, other = shards_of([chip_ref], query_ref.shape[0])
    sets = [
        (own, query_ref, top_ref, sums_ref),
        (other, other_query_ref, other_top_ref, other_sums_ref),
    ]
    for ref in fresh:
        add_shards(sets, ref)


def late_stage(chip_ref, query_ref, other_query_ref, top_ref, other_top_ref, *refs):
    ref, _, _, sums_ref, other_sums_ref = refs
    own, other = shards_of([chip_ref], query_ref.shape[0])
    sets = [
        (own, query_ref, top_ref, sums_ref),
        (other, other_query_ref, other_top_ref, other_sums_ref),
    ]
    add_shards(sets, ref, gets_last())


def repair(query_shard, near, refs, query_ref, top_ref, sums_ref, then=None):
    tokens = query_ref.shape[0]
    heads = query_ref.shape[1] // HEAD_DIM
    largest = functools.reduce(
        jnp.maximum, [sums_ref[head, :, HEAD_DIM:] for head in range(heads)]
    )

    @pl.when(jnp.logical_not(jnp.max(largest) < SAFE_SUM))
    def _():
        far = [(shard, None) for shard in shards_of(refs, tokens)]
        if near is not None:
            far = [(near, is_later())] + far

        def one_head(head, carried):
            query = query_ref[:, pl.ds(pl.multiple_of(head * HEAD_DIM, HEAD_DIM), HEAD_DIM)]
            for shard, usable in far:
                keys, _ = keys_and_values([shard], tokens)
                rows = penalties(query_shard, [shard], tokens, usable)
                scores = scaled_scores(query, keys)
                for query_block, row in enumerate(rows):
                    some = slice(query_block * BLK, (query_block + 1) * BLK)
                    top = top_ref[head, some]
                    for k, gap in enumerate(row):
                        seen = jnp.max(scores[some, columns(k)] - gap, axis=1, keepdims=True)
                        top = jnp.maximum(top, jnp.ceil(seen))
                    top_ref[head, some] = top
            top = top_ref[head]
            sums = jnp.zeros((tokens, 2 * HEAD_DIM), jnp.float32)
            if near is not None:
                keys, values = keys_and_values([query_shard], tokens)
                scores = scaled_scores(query, keys) + causal_bias(query_shard, tokens)
                weights = near_weights(scores, top, tokens)
                sums += jnp.dot(weights, values, preferred_element_type=jnp.float32)
            for shard, usable in far:
                keys, values = keys_and_values([shard], tokens)
                rows = penalties(query_shard, [shard], tokens, usable)
                weights = weights_of(scaled_scores(query, keys), top, rows)
                sums += jnp.dot(weights, values, preferred_element_type=jnp.float32)
            sums_ref[head] = sums
            return carried

        lax.fori_loop(0, heads, one_head, 0)
        if then is not None:
            then()


def side_lanes(top_ref, sums_ref, tokens):
    lane = lax.broadcasted_iota(jnp.int32, (tokens, HEAD_DIM), 1)
    heads = top_ref.shape[0]
    out = jnp.zeros((tokens, HEAD_DIM), jnp.float32)
    for head in range(heads):
        out = jnp.where(lane % HALF == head, sums_ref[head, :, HEAD_DIM:], out)
        out = jnp.where(lane % HALF == heads + head, top_ref[head], out)
    return out


def last_of_other(chip_ref, query_ref, top_in_ref, sums_in_ref, *refs):
    *fresh, out_ref, top_ref, sums_ref = refs
    tokens = query_ref.shape[0]
    heads = query_ref.shape[1] // HEAD_DIM
    _, other = shards_of([chip_ref], tokens)
    sets = [(other, query_ref, top_ref, sums_ref)]
    add_shards(sets, fresh[-2], jnp.logical_not(gets_last()))
    add_shards(sets, fresh[-1])

    def write():
        for head in range(heads):
            out_ref[:, columns(head)] = sums_ref[head, :, :HEAD_DIM].astype(out_ref.dtype)
        side = side_lanes(top_ref, sums_ref, tokens)
        coarse = side.astype(out_ref.dtype).astype(jnp.float32)
        lane = lax.broadcasted_iota(jnp.int32, side.shape, 1)
        side = jnp.where(lane < HALF, coarse, side - coarse)
        out_ref[:, columns(heads)] = side.astype(out_ref.dtype)

    write()
    repair(other, None, fresh, query_ref, top_ref, sums_ref, write)


def last_of_own(chip_ref, query_ref, top_in_ref, sums_in_ref, *refs):
    *fresh, top_ref, sums_ref = refs
    own, other = shards_of([chip_ref], query_ref.shape[0])
    sets = [(own, query_ref, top_ref, sums_ref)]
    add_shards(sets, fresh[-2], jnp.logical_not(gets_last()))
    add_shards(sets, fresh[-1])
    repair(own, other, fresh, query_ref, top_ref, sums_ref)


def merge(top_ref, sums_ref, got_ref, out_ref, semaphores, ready):
    tokens = got_ref.shape[0]
    heads = top_ref.shape[0]
    side = got_ref[:, columns(heads)].astype(jnp.float32)
    side = side + pltpu.roll(side, HALF, 1)
    mine = side_lanes(top_ref, sums_ref, tokens)
    lane = lax.broadcasted_iota(jnp.int32, (tokens, HEAD_DIM), 1)
    apart = jnp.where((lane >= heads) & (lane < 2 * heads), jnp.abs(side - mine), 0.0)
    same = jnp.max(apart) == 0.0

    def spread(lane):
        return jnp.broadcast_to(side[:, lane : lane + 1], (tokens, HEAD_DIM))

    def divide(rescaled):
        for head in range(heads):
            mixture = sums_ref[head, :, :HEAD_DIM]
            row_sum = sums_ref[head, :, HEAD_DIM:]
            got = got_ref[:, columns(head)].astype(jnp.float32)
            got_sum = spread(head)
            if rescaled:
                top = top_ref[head]
                got_top = spread(heads + head)
                highest = jnp.maximum(top, got_top)
                here, there = jnp.exp2(top - highest), jnp.exp2(got_top - highest)
                mixture, row_sum = mixture * here, row_sum * here
                got, got_sum = got * there, got_sum * there
            ready[:, columns(head)] = ((mixture + got) / (row_sum + got_sum)).astype(ready.dtype)
            one_copy(head).start()

    def one_copy(head):
        at = columns(head)
        return pltpu.make_async_copy(ready.at[:, at], out_ref.at[:, at], semaphores.at[head])

    def wait():
        for head in range(heads):
            one_copy(head).wait()

    divide(False)
    wait()

    @pl.when(jnp.logical_not(same))
    def _():
        divide(True)
        wait()


VMEM = pl.BlockSpec(memory_space=pltpu.VMEM)
HBM = pl.BlockSpec(memory_space=pltpu.HBM)


def in_vmem(*arrays):
    return [pltpu.with_memory_space_constraint(one, pltpu.VMEM) for one in arrays]


def call(body, out_shape, operands, aliases=None):
    return pl.pallas_call(
        body,
        out_shape=out_shape,
        in_specs=[VMEM] * len(operands),
        out_specs=jax.tree.map(lambda _: VMEM, out_shape),
        input_output_aliases=aliases or {},
        compiler_params=pltpu.CompilerParams(vmem_limit_bytes=40 << 20),
        cost_estimate=pl.CostEstimate(flops=1, bytes_accessed=1, transcendentals=0),
        name=body.__name__,
    )(*in_vmem(*operands))


def local(queries, keys, values, block_doc):
    tokens, width = queries.shape
    heads = width // HEAD_DIM
    inner_size = lax.axis_size("inner")
    count = lax.axis_size("outer") * inner_size
    assert count % PLANE == 0 and tokens % BLK == 0
    assert (DOC_BLOCKS - 1) * BLK <= 2 * PLANE * tokens
    position = lax.axis_index("outer") * inner_size + lax.axis_index("inner")
    place = position // PAIR % (PLANE // PAIR)
    later = position % PAIR == 1

    def send(array, target):
        route = [(d, target(d)) for d in range(count)]
        return lax.ppermute(array, AXES, [(a, b) for a, b in route if b is not None and b < count])

    def swapped(array):
        return send(array, lambda d: d ^ 1)

    def flipped(d, flip):
        return d ^ (PAIR * flip)

    payload = pl.pallas_call(
        pack,
        out_shape=pltpu.VMEM((shard_rows(tokens), HEAD_DIM), keys.dtype),
        in_specs=[HBM] * 3,
        out_specs=VMEM,
        scratch_shapes=[
            pltpu.SMEM(block_doc.shape, block_doc.dtype),
            pltpu.SemaphoreType.DMA((3,)),
        ],
        name="pack",
    )(block_doc, keys, values)
    chip = jnp.concatenate([payload, swapped(payload)], axis=0)
    other_queries = swapped(queries)

    def straight(d, flip):
        if d % PAIR == 0:
            return flipped(d, flip) + PLANE
        return flipped(d, flip) if flipped(d, flip) > d else flipped(d, flip) + 2 * PLANE if flip == 0 else None

    far = send(chip, lambda d: straight(d, 0))
    across = send(chip, lambda d: straight(d, 3))

    top_shape = pltpu.VMEM((heads, tokens, HEAD_DIM), jnp.float32)
    sums_shape = pltpu.VMEM((heads, tokens, 2 * HEAD_DIM), jnp.float32)
    top, other_top, sums, other_sums = call(
        first_stage,
        (top_shape, top_shape, sums_shape, sums_shape),
        (chip, queries, other_queries),
    )

    def add(sums, *fresh, stage=middle_stage):
        operands = (chip, queries, other_queries, top, other_top, *fresh, *sums)
        at = len(operands) - 2
        return call(stage, (sums_shape, sums_shape), operands, {at: 0, at + 1: 1})

    far, both = lax.optimization_barrier((far, (sums, other_sums)))

    def beside(step):
        before = place & jnp.where(later, 3 - step, step) == 0
        passed = jnp.where(later & before, chip, far)
        return send(passed, lambda d: flipped(d, 3 - step if d % PAIR else step))

    last = send(far, lambda d: flipped(d, 3) if d % PAIR and flipped(d, 3) < d else None)
    received = (far, across, beside(1), beside(2), last)
    for one in received[:-2]:
        both = add(both, one)
    sums, other_sums = add(both, received[-2], stage=late_stage)
    message, _, _ = call(
        last_of_other,
        (pltpu.VMEM((tokens, width + HEAD_DIM), queries.dtype), top_shape, sums_shape),
        (chip, other_queries, other_top, other_sums, *received),
        {2: 1, 3: 2},
    )
    got = swapped(message)
    top, sums = call(
        last_of_own,
        (top_shape, sums_shape),
        (chip, queries, top, sums, *received),
        {2: 0, 3: 1},
    )
    return pl.pallas_call(
        merge,
        out_shape=jax.ShapeDtypeStruct(queries.shape, queries.dtype),
        in_specs=[VMEM] * 3,
        out_specs=HBM,
        scratch_shapes=[
            pltpu.SemaphoreType.DMA((heads,)),
            pltpu.VMEM(queries.shape, queries.dtype),
        ],
        compiler_params=pltpu.CompilerParams(vmem_limit_bytes=40 << 20),
        name="merge",
    )(*in_vmem(top, sums, got))


def solution(mesh):
    placed = (
        P(AXES, None),
        P(AXES, None),
        P(AXES, None),
        P(AXES),
    )
    return jax.shard_map(
        local, mesh=mesh, in_specs=placed, out_specs=P(AXES, None), check_vma=False
    )
```
